512 devices in a mesh: rows: 64 (over x, z, core), grp: 8 (over y).
Axes of the slice: x: 4, y: 8, z: 8, core: 2. Of those that a mesh axis runs over, the one named last changes fastest.
Arguments:
- matrix: float32 [131072, 768], P(('rows', 'grp')), as said below
- sketch: float32 [768, 256], replicated, may hold values from -6 to 6
Outputs:
- basis_scaled: float32 [131072, 256], P(('rows', 'grp'))
- coeffs: float32 [256, 768], P(None, 'rows')
The draws below stay inside these ranges and needn't reach their ends.
Inputs may be any that keep to these rules, and one draw needn't show every extreme that they name: Rows of the matrix have independent scales; entries are bounded by 48 / sqrt(131072) in magnitude.
All inputs are finite; a program needn't handle non-finite values.
Results may differ from the reference program's by a relative error of at most 0.0003.
Values sent between devices are 32-bit elements; how exact they have to be, the bound alone decides.
A program may use at most 64 MiB of HBM per device.

```python
import jax
import jax.numpy as jnp
from jax import lax

D = 768
K = 256
ROWS_ALL = 131072


def draw_matrix(key, part):
    key = jax.random.fold_in(key, 7)
    first_key, second_key = jax.random.split(key)
    base = jnp.clip(jax.random.normal(first_key, (ROWS_ALL, D), jnp.float32), -5.0, 5.0)
    spread = 1.15
    rough = jnp.exp(jax.random.uniform(second_key, (ROWS_ALL, 1), jnp.float32, -spread, spread))
    ramp = 1.0 + 2.0 * jnp.arange(ROWS_ALL, dtype=jnp.float32)[:, None] / ROWS_ALL
    return base * rough * ramp / jnp.sqrt(jnp.float32(ROWS_ALL))


def gaussian(stream_key, shape, scale, limit, kind=jnp.bfloat16):
    result = jax.random.normal(stream_key, shape, jnp.float32) * scale
    return jnp.minimum(jnp.maximum(result, -limit), limit).astype(kind)


def setup_inputs(seed: int = 0) -> dict:
    streams_of = jax.random.split(jax.random.key(seed), 3)
    matrix = draw_matrix(jax.random.fold_in(streams_of[2], 71), 0)
    sketch = gaussian(streams_of[1], (D, K), 1.0, 6.0, jnp.float32)
    return dict(matrix=matrix, sketch=sketch)


def mult(left, right):
    return jnp.dot(left.astype(jnp.float32), right.astype(jnp.float32), precision=lax.Precision.HIGHEST, preferred_element_type=jnp.float32)

def reference(matrix, sketch):
    proj = mult(matrix, sketch)
    power = mult(matrix.T, proj)
    range_rows = mult(matrix, power)
    gram = mult(range_rows.T, range_rows)
    lower = jnp.linalg.cholesky(gram)
    basis = jax.scipy.linalg.solve_triangular(lower, range_rows.T, lower=True).T
    coeffs = mult(basis.T, matrix)
    scaled = basis * jnp.sqrt(jnp.float32(ROWS_ALL))
    return (scaled, coeffs)
```

```python
import functools
import jax
import jax.numpy as jnp
from jax import lax
from jax.experimental import pallas as pl
from jax.experimental.pallas import tpu as pltpu
from jax.sharding import PartitionSpec as P

MESH = pl.DeviceIdType.MESH
F32 = jnp.float32
BF16 = jnp.bfloat16
NX, NY, NZ = 4, 8, 8
BLOCKS = [(i, j) for i in range(6) for j in range(i, 6)]
LIVE = 336
HELD = 384
PIECE = 24


def split(v):
    high = v.astype(BF16)
    return high, (v - high.astype(F32)).astype(BF16)


NN = (((1,), (0,)), ((), ()))
NT = (((1,), (1,)), ((), ()))
TN = (((0,), (0,)), ((), ()))


def dot3(left, right, dims):
    def one(a, b):
        return lax.dot_general(a, b, dims, preferred_element_type=F32)
    return one(left[0], right[1]) + one(left[1], right[0]) + one(left[0], right[0])


def place(tile):
    share, row = divmod(tile, LIVE // 8)
    return share // NX, share % NX, row * 8


def store_block(part, index, value):
    for t in range(16):
        core, x, row = place(index * 16 + t)
        part[core, x, row:row + 8, :] = value[8 * t:8 * t + 8, :]


def reduce_kernel(a_hbm, g_ref, a_own, part, sib_in, x_in, acc, z_in, y_in, zy, yz, gath,
                  load_sem, sib_s, sib_r, x_s, x_r, z_s, z_r, y_s, y_r, zy_s, zy_r, yz_s, yz_r,
                  zg_s, zg_r, yg_s, yg_r, xg_s, xg_r, fw_s, fw_r):
    r = lax.axis_index("rows")
    y = lax.axis_index("grp")
    x, z, c = r // 16, lax.rem(r // 2, 8), lax.rem(r, 2)

    def dev(xx, yy, zz, cc):
        return ((xx * NZ + zz) * 2 + cc, yy)

    def other(axis, k):
        if axis == "x":
            return lax.rem(x + k, NX), dev(lax.rem(x + k, NX), y, z, c)
        if axis == "y":
            return lax.rem(y + k, NY), dev(x, lax.rem(y + k, NY), z, c)
        return lax.rem(z + k, NZ), dev(x, y, lax.rem(z + k, NZ), c)

    sibling = dev(x, y, z, 1 - c)
    barrier = pltpu.get_barrier_semaphore()
    pl.semaphore_signal(barrier, inc=1, device_id=sibling, device_id_type=MESH)
    for axis, n in (("x", NX), ("y", NY), ("z", NZ)):
        for k in range(1, n):
            pl.semaphore_signal(barrier, inc=1, device_id=other(axis, k)[1], device_id_type=MESH)
    load = pltpu.make_async_copy(a_hbm, a_own, load_sem)
    load.start()
    load.wait()

    def copy(src, dst, s, rr, to):
        return pltpu.make_async_remote_copy(src_ref=src, dst_ref=dst, send_sem=s, recv_sem=rr,
                                            device_id=to, device_id_type=MESH)

    halves = [split(a_own[:, 128 * i:128 * i + 128]) for i in range(6)]
    for index, (i, j) in enumerate(BLOCKS):
        store_block(part, index, dot3(halves[i], halves[j], TN))

    pl.semaphore_wait(barrier, 1 + (NX - 1) + (NY - 1) + (NZ - 1))
    sent = []
    live = pl.ds(0, LIVE)

    swaps = []
    for k in (1, 2, 3, 0):
        xx = lax.rem(x + k, NX)
        d = copy(part.at[1 - c, xx, live], sib_in.at[xx], sib_s.at[xx], sib_r.at[xx], sibling)
        d.start()
        swaps.append((xx, d))
        sent.append(d)
    for (xx, d), k in zip(swaps[:3], (1, 2, 3)):
        d.wait_recv()
        part[c, xx, 0:LIVE, :] = part[c, xx, 0:LIVE, :] + sib_in[xx]
        out = copy(part.at[c, xx, live], x_in.at[k - 1], x_s.at[k - 1], x_r.at[k - 1], other("x", k)[1])
        out.start()
        sent.append(out)
    swaps[3][1].wait_recv()
    for k in (1, 2, 3):
        copy(part.at[c, x, live], x_in.at[k - 1], x_s.at[k - 1], x_r.at[k - 1], sibling).wait_recv()
    acc[0:LIVE, :] = (part[c, x, 0:LIVE, :] + sib_in[x]) + (x_in[0] + x_in[1] + x_in[2])
    acc[LIVE:HELD, :] = jnp.zeros((HELD - LIVE, 128), F32)

    def piece(half, owner):
        return pl.ds(pl.multiple_of(half * (HELD // 2) + owner * PIECE, 8), PIECE)

    for k in range(1, 8):
        zz, to = other("z", k)
        d = copy(acc.at[piece(0, zz)], z_in.at[k - 1], z_s.at[k - 1], z_r.at[k - 1], to)
        d.start()
        yy, to = other("y", k)
        e = copy(acc.at[piece(1, yy)], y_in.at[k - 1], y_s.at[k - 1], y_r.at[k - 1], to)
        e.start()
        sent += [d, e]
    zsum = acc[piece(0, z), :]
    ysum = acc[piece(1, y), :]
    for k in range(1, 8):
        copy(acc.at[piece(0, z)], z_in.at[k - 1], z_s.at[k - 1], z_r.at[k - 1], sibling).wait_recv()
        zsum += z_in[k - 1]
    zy[y] = zsum
    for k in range(1, 8):
        _, to = other("y", k)
        d = copy(zy.at[y], zy.at[y], zy_s.at[k - 1], zy_r.at[y], to)
        d.start()
        sent.append(d)
    for k in range(1, 8):
        copy(acc.at[piece(1, y)], y_in.at[k - 1], y_s.at[k - 1], y_r.at[k - 1], sibling).wait_recv()
        ysum += y_in[k - 1]
    yz[z] = ysum
    for k in range(1, 8):
        _, to = other("z", k)
        d = copy(yz.at[z], yz.at[z], yz_s.at[k - 1], yz_r.at[z], to)
        d.start()
        sent.append(d)
    for k in range(1, 8):
        yy, _ = other("y", k)
        copy(zy.at[yy], zy.at[yy], zy_s.at[k - 1], zy_r.at[yy], sibling).wait_recv()
    mine = gath.at[c, x]
    total = zy[0]
    for k in range(1, 8):
        total += zy[k]
    gath[c, x, piece(0, z), :] = total
    for k in range(1, 8):
        _, to = other("z", k)
        d = copy(mine.at[piece(0, z)], mine.at[piece(0, z)], zg_s.at[k - 1], zg_r.at[z], to)
        d.start()
        sent.append(d)
    for k in range(1, 8):
        zz, _ = other("z", k)
        copy(yz.at[zz], yz.at[zz], yz_s.at[k - 1], yz_r.at[zz], sibling).wait_recv()
    total = yz[0]
    for k in range(1, 8):
        total += yz[k]
    gath[c, x, piece(1, y), :] = total
    for k in range(1, 8):
        _, to = other("y", k)
        d = copy(mine.at[piece(1, y)], mine.at[piece(1, y)], yg_s.at[k - 1], yg_r.at[y], to)
        d.start()
        sent.append(d)
    for k in range(1, 8):
        zz, _ = other("z", k)
        copy(mine.at[piece(0, zz)], mine.at[piece(0, zz)], zg_s.at[k - 1], zg_r.at[zz], sibling).wait_recv()
    for k in range(1, 8):
        yy, _ = other("y", k)
        copy(mine.at[piece(1, yy)], mine.at[piece(1, yy)], yg_s.at[k - 1], yg_r.at[yy], sibling).wait_recv()

    quarter = gath.at[c, x, live]
    for k in (1, 2, 3):
        d = copy(quarter, quarter, xg_s.at[k - 1], xg_r.at[x], other("x", k)[1])
        d.start()
        sent.append(d)
    d = copy(quarter, quarter, fw_s.at[x], fw_r.at[x], sibling)
    d.start()
    sent.append(d)
    for k in (1, 3, 2):
        xx, _ = other("x", k)
        came = gath.at[c, xx, live]
        copy(came, came, xg_s.at[k - 1], xg_r.at[xx], sibling).wait_recv()
        d = copy(came, came, fw_s.at[xx], fw_r.at[xx], sibling)
        d.start()
        sent.append(d)
    for xx in range(NX):
        came = gath.at[1 - c, xx, live]
        copy(came, came, fw_s.at[xx], fw_r.at[xx], sibling).wait_recv()
    g_ref[...] = gath[:, :, 0:LIVE, :]
    for d in sent:
        d.wait_send()


def dma(*shape):
    return pltpu.SemaphoreType.DMA(shape)


def reduced_gram(matrix):
    rows, cols = matrix.shape
    return pl.pallas_call(
        reduce_kernel,
        out_shape=jax.ShapeDtypeStruct((2, NX, LIVE, 128), F32),
        in_specs=[pl.BlockSpec(memory_space=pl.ANY)],
        out_specs=pl.BlockSpec(memory_space=pltpu.VMEM),
        scratch_shapes=[
            pltpu.VMEM((rows, cols), F32),
            pltpu.VMEM((2, NX, HELD, 128), F32),
            pltpu.VMEM((NX, LIVE, 128), F32),
            pltpu.VMEM((NX - 1, LIVE, 128), F32),
            pltpu.VMEM((HELD, 128), F32),
            pltpu.VMEM((7, PIECE, 128), F32),
            pltpu.VMEM((7, PIECE, 128), F32),
            pltpu.VMEM((8, PIECE, 128), F32),
            pltpu.VMEM((8, PIECE, 128), F32),
            pltpu.VMEM((2, NX, HELD, 128), F32),
            pltpu.SemaphoreType.DMA,
            dma(4), dma(4), dma(3), dma(3), dma(7), dma(7), dma(7), dma(7),
            dma(7), dma(8), dma(7), dma(8), dma(7), dma(8), dma(7), dma(8),
            dma(3), dma(4), dma(4), dma(4),
        ],
        compiler_params=pltpu.CompilerParams(collective_id=0, has_side_effects=True,
                                             vmem_limit_bytes=40 * 1024 * 1024),
        name="reduce_gram",
    )(matrix)


def panel_inverse_8(d, nb):
    n8 = nb // 8
    eye = (lax.broadcasted_iota(jnp.int32, (nb, nb), 0) == lax.broadcasted_iota(jnp.int32, (nb, nb), 1)).astype(F32)
    w = jnp.concatenate([d, eye], 1)
    groups = [w[8 * g:8 * g + 8, :] for g in range(n8)]
    sub = lax.broadcasted_iota(jnp.int32, (8, 128), 0)
    out = [None] * n8
    for g in range(n8):
        cols = {h: [jnp.broadcast_to(groups[h][:, 8 * g + k:8 * g + k + 1], (8, 128)) for k in range(8)] for h in range(g, n8)}
        pivots = []
        for k in range(8):
            row = jnp.broadcast_to(groups[g][k:k + 1, :], (8, 128))
            rows = {m: jnp.broadcast_to(cols[g][m][k:k + 1, :], (8, 128)) for m in range(k, 8)}
            inv = 1.0 / rows[k]
            pivots.append(rows[k])
            q = row * inv
            qs = {m: rows[m] * inv for m in range(k + 1, 8)}
            for h in range(g, n8):
                c = cols[h][k]
                if h == g:
                    c = jnp.where(sub > k, c, 0.0)
                groups[h] = groups[h] - c * q
                for m in range(k + 1, 8):
                    cols[h][m] = cols[h][m] - c * qs[m]
        dia = pivots[7]
        for k in range(7):
            dia = jnp.where(sub == k, pivots[k], dia)
        out[g] = groups[g][:, nb:] * lax.rsqrt(dia)[:, nb:]
    return jnp.concatenate(out, 0)


def cholesky_inverse(gram, linv, nb, panel):
    n = gram.shape[0]
    linv[...] = jnp.zeros((n, n), F32)
    for b in range(n // nb):
        lo, hi = b * nb, (b + 1) * nb
        x = panel(gram[lo:hi, lo:hi], nb)
        xs = split(x)
        if b:
            done = dot3(xs, split(linv[lo:hi, 0:lo]), NN)
            linv[lo:hi, 0:lo] = done
        linv[lo:hi, lo:hi] = x
        if hi < n:
            u = split(dot3(xs, split(gram[lo:hi, hi:n]), NN))
            gram[hi:n, hi:n] = gram[hi:n, hi:n] - dot3(u, u, TN)
            linv[hi:n, 0:hi] = linv[hi:n, 0:hi] - dot3(u, split(linv[lo:hi, 0:hi]), TN)


def load_block(packed, index):
    pieces = []
    for t in range(16):
        core, x, row = place(index * 16 + t)
        pieces.append(packed[core, x, row:row + 8, :])
    return jnp.concatenate(pieces, 0)


def times_gram(left, high, low, dims_of=None):
    strips = []
    for s in range(3):
        lo, hi = 256 * s, 256 * s + 256
        strip = dot3((left[0][:, :hi], left[1][:, :hi]), (high[0:hi, lo:hi], low[0:hi, lo:hi]), NN)
        if hi < 768:
            strip += dot3((left[0][:, hi:], left[1][:, hi:]), (high[lo:hi, hi:], low[lo:hi, hi:]), NT)
        strips.append(strip)
    return jnp.concatenate(strips, 1)


def finish_kernel(scale, packed, a_ref, s_ref, basis_ref, coeffs_ref, high, low, gram, linv):
    r = lax.axis_index("rows")
    for index, (i, j) in enumerate(BLOCKS):
        block = load_block(packed, index)
        h, l = split(block)
        high[128 * i:128 * i + 128, 128 * j:128 * j + 128] = h
        low[128 * i:128 * i + 128, 128 * j:128 * j + 128] = l
        if i // 2 == j // 2 and i != j:
            h, l = split(block.T)
            high[128 * j:128 * j + 128, 128 * i:128 * i + 128] = h
            low[128 * j:128 * j + 128, 128 * i:128 * i + 128] = l
    power = split(times_gram(split(s_ref[...].T), high, low))
    ranged = times_gram(power, high, low)
    halves = split(ranged)
    gram[...] = dot3(halves, power, NT)
    cholesky_inverse(gram, linv, 64, panel_inverse_8)
    inverse = split(linv[...])
    factor = split(dot3(inverse, power, NN))
    basis_ref[...] = dot3(split(a_ref[...]), factor, NT) * scale
    width = coeffs_ref.shape[1]
    row = lax.broadcasted_iota(jnp.int32, (768, 128), 0)
    col = lax.broadcasted_iota(jnp.int32, (768, 128), 1)
    pick = jnp.where(row == col + r * width, 1.0, 0.0).astype(BF16)
    rest = (ranged - halves[0].astype(F32)) - halves[1].astype(F32)
    mine = sum(lax.dot_general(part, pick, NN, preferred_element_type=F32)
               for part in (halves[0], halves[1], rest.astype(BF16)))
    coeffs_ref[...] = dot3(inverse, split(mine), NN)[:, 0:width]


def finish(packed, matrix, sketch, scale, width):
    vmem = pl.BlockSpec(memory_space=pltpu.VMEM)
    return pl.pallas_call(
        functools.partial(finish_kernel, scale),
        out_shape=(jax.ShapeDtypeStruct((256, 256), F32), jax.ShapeDtypeStruct((256, width), F32)),
        in_specs=[vmem] * 3,
        out_specs=(vmem, vmem),
        scratch_shapes=[
            pltpu.VMEM((768, 768), BF16),
            pltpu.VMEM((768, 768), BF16),
            pltpu.VMEM((256, 256), F32),
            pltpu.VMEM((256, 256), F32),
        ],
        compiler_params=pltpu.CompilerParams(vmem_limit_bytes=40 * 1024 * 1024),
        name="finish",
    )(packed, matrix, sketch)


def shards(matrix, sketch):
    parts = lax.axis_size("rows") * lax.axis_size("grp")
    packed = reduced_gram(matrix)
    scale = float((matrix.shape[0] * parts) ** 0.5)
    return finish(packed, matrix, sketch, scale, matrix.shape[1] // lax.axis_size("rows"))


def solution(mesh):
    return jax.shard_map(
        shards,
        mesh=mesh,
        in_specs=(P(("rows", "grp"), None), P()),
        out_specs=(P(("rows", "grp"), None), P(None, "rows")),
        check_vma=False,
    )
```

```python
import functools
import jax
import jax.numpy as jnp
from jax import lax
from jax.experimental import pallas as pl
from jax.experimental.pallas import tpu as pltpu
from jax.sharding import PartitionSpec as P

MESH = pl.DeviceIdType.MESH
F32 = jnp.float32
BF16 = jnp.bfloat16
NX, NY, NZ = 4, 8, 8
BLOCKS = [(i, j) for i in range(6) for j in range(i, 6)]
LIVE = 336
HELD = 384
PIECE = 24


def split(v):
    high = v.astype(BF16)
    return high, (v - high.astype(F32)).astype(BF16)


NN = (((1,), (0,)), ((), ()))
NT = (((1,), (1,)), ((), ()))
TN = (((0,), (0,)), ((), ()))


def dot3(left, right, dims):
    def one(a, b):
        return lax.dot_general(a, b, dims, preferred_element_type=F32)
    return one(left[0], right[1]) + one(left[1], right[0]) + one(left[0], right[0])


def place(tile):
    share, row = divmod(tile, LIVE // 8)
    return share // NX, share % NX, row * 8


def store_block(part, index, value):
    for t in range(16):
        core, x, row = place(index * 16 + t)
        part[core, x, row:row + 8, :] = value[8 * t:8 * t + 8, :]


PARTS = (pl.ds(0, HELD // 2), pl.ds(HELD // 2, LIVE - HELD // 2))


def reduce_kernel(a_hbm, high, low, a_own, part, sib_in, x_in, acc, z_in, y_in, zy, yz, gath, load_sem,
                  sib_s, sib_r, x_s, x_r, z_s, z_r, y_s, y_r, zy_s, zy_r, yz_s, yz_r,
                  zg_s, zg_r, yg_s, yg_r, xg_s, xg_r, fw_s, fw_r):
    r = lax.axis_index("rows")
    y = lax.axis_index("grp")
    x, z, c = r // 16, lax.rem(r // 2, 8), lax.rem(r, 2)

    def dev(xx, yy, zz, cc):
        return ((xx * NZ + zz) * 2 + cc, yy)

    def other(axis, k):
        if axis == "x":
            return lax.rem(x + k, NX), dev(lax.rem(x + k, NX), y, z, c)
        if axis == "y":
            return lax.rem(y + k, NY), dev(x, lax.rem(y + k, NY), z, c)
        return lax.rem(z + k, NZ), dev(x, y, lax.rem(z + k, NZ), c)

    sibling = dev(x, y, z, 1 - c)
    load = pltpu.make_async_copy(a_hbm, a_own, load_sem)
    load.start()
    barrier = pltpu.get_barrier_semaphore()
    for axis, n in (("x", NX), ("y", NY), ("z", NZ)):
        for k in range(1, n):
            pl.semaphore_signal(barrier, inc=1, device_id=other(axis, k)[1], device_id_type=MESH)
    pl.semaphore_signal(barrier, inc=1, device_id=sibling, device_id_type=MESH)

    def copy(src, dst, s, rr, to=sibling):
        return pltpu.make_async_remote_copy(src_ref=src, dst_ref=dst, send_sem=s, recv_sem=rr,
                                            device_id=to, device_id_type=MESH)

    sent = []

    def send(*args):
        d = copy(*args)
        d.start()
        sent.append(d)

    load.wait()
    halves = split(a_own[...])
    for i in range(6):
        lo = 128 * i
        strip = dot3((halves[0][:, lo:lo + 128], halves[1][:, lo:lo + 128]), (halves[0][:, lo:], halves[1][:, lo:]), TN)
        for j in range(i, 6):
            store_block(part, BLOCKS.index((i, j)), strip[:, 128 * j - lo:128 * j - lo + 128])

    pl.semaphore_wait(barrier, 1 + (NX - 1) + (NY - 1) + (NZ - 1))

    order = (2, 1, 3, 0)
    quarters = [lax.rem(x + k, NX) for k in order]
    for h, rows in enumerate(PARTS):
        for xx in quarters:
            send(part.at[1 - c, xx, rows], sib_in.at[xx, rows], sib_s.at[h, xx], sib_r.at[h, xx], sibling)
    for h, rows in enumerate(PARTS):
        for k, xx in zip(order, quarters):
            copy(part.at[1 - c, xx, rows], sib_in.at[xx, rows], sib_s.at[h, xx], sib_r.at[h, xx]).wait_recv()
            part[c, xx, rows, :] = part[c, xx, rows, :] + sib_in[xx, rows, :]
            if k:
                send(part.at[c, xx, rows], x_in.at[k - 1, rows], x_s.at[h, k - 1], x_r.at[h, k - 1], other("x", k)[1])
    acc[LIVE:HELD, :] = jnp.zeros((HELD - LIVE, 128), F32)

    def piece(half, owner):
        return pl.ds(pl.multiple_of(half * (HELD // 2) + owner * PIECE, 8), PIECE)

    along = (("z", z, z_in, z_s, z_r), ("y", y, y_in, y_s, y_r))
    for h, (axis, me, box, ss, rs) in enumerate(along):
        rows = PARTS[h]
        for k in (1, 3, 2):
            copy(part.at[c, x, rows], x_in.at[k - 1, rows], x_s.at[h, k - 1], x_r.at[h, k - 1]).wait_recv()
        acc[rows, :] = part[c, x, rows, :] + (x_in[0, rows, :] + x_in[1, rows, :] + x_in[2, rows, :])
        for k in (4, 3, 5, 2, 6, 1, 7):
            to, device = other(axis, k)
            send(acc.at[piece(h, to)], box.at[k - 1], ss.at[k - 1], rs.at[k - 1], device)
    cross = (("y", y, zy, zy_s, zy_r), ("z", z, yz, yz_s, yz_r))
    for h, (axis, me, box, ss, rs) in enumerate(along):
        for k in range(1, 8):
            copy(acc.at[piece(h, me)], box.at[k - 1], ss.at[k - 1], rs.at[k - 1]).wait_recv()
        total = acc[piece(h, me), :]
        for k in range(1, 8):
            total += box[k - 1]
        axis, me, box, ss, rs = cross[h]
        box[me] = total
        for k in (4, 3, 5, 2, 6, 1, 7):
            send(box.at[me], box.at[me], ss.at[k - 1], rs.at[me], other(axis, k)[1])
    mine = gath.at[c, x]
    back = (("z", z, zg_s, zg_r), ("y", y, yg_s, yg_r))
    for h, (axis, me, box, ss, rs) in enumerate(cross):
        for k in range(1, 8):
            at, _ = other(axis, k)
            copy(box.at[at], box.at[at], ss.at[k - 1], rs.at[at]).wait_recv()
        total = box[0]
        for k in range(1, 8):
            total += box[k]
        axis, me, ss, rs = back[h]
        gath[c, x, piece(h, me), :] = total
        for k in (4, 3, 5, 2, 6, 1, 7):
            send(mine.at[piece(h, me)], mine.at[piece(h, me)], ss.at[k - 1], rs.at[me], other(axis, k)[1])
    def halve(core, xx, h):
        share = core * NX + xx
        for n in range(PARTS[h].size // 16):
            row = PARTS[h].start + 16 * n
            high[share, row:row + 16, :], low[share, row:row + 16, :] = split(gath[core, xx, row:row + 16, :])

    for h, (axis, me, ss, rs) in enumerate(back):
        for k in range(1, 8):
            at, _ = other(axis, k)
            copy(mine.at[piece(h, at)], mine.at[piece(h, at)], ss.at[k - 1], rs.at[at]).wait_recv()
        rows = PARTS[h]
        quarter = gath.at[c, x, rows]
        for k in (2, 1, 3):
            send(quarter, quarter, xg_s.at[h, k - 1], xg_r.at[h, x], other("x", k)[1])
        send(quarter, quarter, fw_s.at[h, x], fw_r.at[h, x], sibling)
        halve(c, x, h)
    for h, rows in enumerate(PARTS):
        for k in (1, 3, 2):
            xx, _ = other("x", k)
            came = gath.at[c, xx, rows]
            copy(came, came, xg_s.at[h, k - 1], xg_r.at[h, xx]).wait_recv()
            send(came, came, fw_s.at[h, xx], fw_r.at[h, xx], sibling)
            halve(c, xx, h)
    for h, rows in enumerate(PARTS):
        for k in (0, 1, 3, 2):
            xx, _ = other("x", k)
            came = gath.at[1 - c, xx, rows]
            copy(came, came, fw_s.at[h, xx], fw_r.at[h, xx]).wait_recv()
            halve(1 - c, xx, h)
    for d in sent:
        d.wait_send()


def dma(*shape):
    return pltpu.SemaphoreType.DMA(shape)


def reduced_gram(matrix):
    rows, cols = matrix.shape
    vmem = pl.BlockSpec(memory_space=pltpu.VMEM)
    return pl.pallas_call(
        reduce_kernel,
        out_shape=[jax.ShapeDtypeStruct((2 * NX, LIVE, 128), BF16)] * 2,
        in_specs=[pl.BlockSpec(memory_space=pltpu.HBM)],
        out_specs=[vmem] * 2,
        scratch_shapes=[
            pltpu.VMEM((rows, cols), F32),
            pltpu.VMEM((2, NX, HELD, 128), F32),
            pltpu.VMEM((NX, LIVE, 128), F32),
            pltpu.VMEM((NX - 1, LIVE, 128), F32),
            pltpu.VMEM((HELD, 128), F32),
            pltpu.VMEM((7, PIECE, 128), F32),
            pltpu.VMEM((7, PIECE, 128), F32),
            pltpu.VMEM((8, PIECE, 128), F32),
            pltpu.VMEM((8, PIECE, 128), F32),
            pltpu.VMEM((2, NX, HELD, 128), F32),
            pltpu.SemaphoreType.DMA,
            dma(2, 4), dma(2, 4), dma(2, 3), dma(2, 3), dma(7), dma(7), dma(7), dma(7),
            dma(7), dma(8), dma(7), dma(8), dma(7), dma(8), dma(7), dma(8),
            dma(2, 3), dma(2, 4), dma(2, 4), dma(2, 4),
        ],
        compiler_params=pltpu.CompilerParams(collective_id=0, has_side_effects=True,
                                             vmem_limit_bytes=40 * 1024 * 1024),
        name="reduce_gram",
    )(matrix)


def panel_inverse_8(d, nb):
    n8 = nb // 8
    eye = (lax.broadcasted_iota(jnp.int32, (nb, nb), 0) == lax.broadcasted_iota(jnp.int32, (nb, nb), 1)).astype(F32)
    w = jnp.concatenate([d, eye], 1)
    groups = [w[8 * g:8 * g + 8, :] for g in range(n8)]
    sub = lax.broadcasted_iota(jnp.int32, (8, 128), 0)
    out = [None] * n8
    for g in range(n8):
        cols = {h: [jnp.broadcast_to(groups[h][:, 8 * g + k:8 * g + k + 1], (8, 128)) for k in range(8)] for h in range(g, n8)}
        pivots = []
        for k in range(8):
            row = jnp.broadcast_to(groups[g][k:k + 1, :], (8, 128))
            rows = {m: jnp.broadcast_to(cols[g][m][k:k + 1, :], (8, 128)) for m in range(k, 8)}
            inv = 1.0 / rows[k]
            pivots.append(rows[k])
            q = row * inv
            qs = {m: rows[m] * inv for m in range(k + 1, 8)}
            for h in range(g, n8):
                c = cols[h][k]
                if h == g:
                    c = jnp.where(sub > k, c, 0.0)
                groups[h] = groups[h] - c * q
                for m in range(k + 1, 8):
                    cols[h][m] = cols[h][m] - c * qs[m]
        dia = pivots[7]
        for k in range(7):
            dia = jnp.where(sub == k, pivots[k], dia)
        out[g] = groups[g][:, nb:] * lax.rsqrt(dia)[:, nb:]
    return jnp.concatenate(out, 0)


def cholesky_inverse(gram, linv, nb, panel):
    n = gram.shape[0]
    linv[...] = jnp.zeros((n, n), F32)
    for b in range(n // nb):
        lo, hi = b * nb, (b + 1) * nb
        x = panel(gram[lo:hi, lo:hi], nb)
        xs = split(x)
        if b:
            done = dot3(xs, split(linv[lo:hi, 0:lo]), NN)
            linv[lo:hi, 0:lo] = done
        linv[lo:hi, lo:hi] = x
        if hi < n:
            u = split(dot3(xs, split(gram[lo:hi, hi:n]), NN))
            gram[hi:n, hi:n] = gram[hi:n, hi:n] - dot3(u, u, TN)
            linv[hi:n, 0:hi] = linv[hi:n, 0:hi] - dot3(u, split(linv[lo:hi, 0:hi]), TN)


def upper(ref, i, j):
    at = 128 * BLOCKS.index((i, j))
    return ref[at:at + 128, :]


def gram_strips(ref, corners):
    strips = []
    for s in range(3):
        p, q = 2 * s, 2 * s + 1
        above = [jnp.concatenate([upper(ref, i, p), upper(ref, i, q)], 1) for i in range(q)]
        above.append(jnp.concatenate([corners[s], upper(ref, q, q)], 1))
        right = None
        if s < 2:
            right = jnp.concatenate([jnp.concatenate([upper(ref, i, j) for j in range(q + 1, 6)], 1) for i in (p, q)], 0)
        strips.append((jnp.concatenate(above, 0), right))
    return strips


def times_gram(left, high, low):
    out = []
    for s in range(3):
        hi = 256 * s + 256
        strip = dot3((left[0][:, :hi], left[1][:, :hi]), (high[s][0], low[s][0]), NN)
        if s < 2:
            strip += dot3((left[0][:, hi:], left[1][:, hi:]), (high[s][1], low[s][1]), NT)
        out.append(strip)
    return jnp.concatenate(out, 1)


def finish_kernel(scale, g_high, g_low, matrix, sketch, basis_ref, coeffs_ref, gram, linv):
    r = lax.axis_index("rows")
    high, low = (gram_strips(ref, [upper(ref, 2 * s, 2 * s + 1).T for s in range(3)]) for ref in (g_high, g_low))
    power = split(times_gram(split(sketch[...].T), high, low))
    ranged = times_gram(power, high, low)
    halves = split(ranged)
    gram[...] = dot3(halves, power, NT)
    cholesky_inverse(gram, linv, 64, panel_inverse_8)
    inverse = split(linv[...])
    factor = split(dot3(inverse, power, NN))
    basis_ref[...] = dot3(split(matrix[...]), factor, NT) * scale
    width = coeffs_ref.shape[0]
    row = lax.broadcasted_iota(jnp.int32, (128, 768), 0)
    col = lax.broadcasted_iota(jnp.int32, (128, 768), 1)
    pick = jnp.where(col == row + r * width, 1.0, 0.0).astype(BF16)
    rest = (ranged - halves[0].astype(F32)) - halves[1].astype(F32)
    mine = sum(lax.dot_general(pick, part, NT, preferred_element_type=F32)
               for part in (halves[0], halves[1], rest.astype(BF16)))
    coeffs_ref[...] = dot3(split(mine), inverse, NT)[0:width, :]


def finish(operands, scale, width):
    vmem = pl.BlockSpec(memory_space=pltpu.VMEM)
    return pl.pallas_call(
        functools.partial(finish_kernel, scale),
        out_shape=(jax.ShapeDtypeStruct((256, 256), F32), jax.ShapeDtypeStruct((width, 256), F32)),
        in_specs=[vmem] * 4,
        out_specs=(vmem, vmem),
        scratch_shapes=[pltpu.VMEM((256, 256), F32), pltpu.VMEM((256, 256), F32)],
        compiler_params=pltpu.CompilerParams(vmem_limit_bytes=40 * 1024 * 1024),
        name="finish",
    )(*operands)


def shards(matrix, sketch):
    parts = lax.axis_size("rows") * lax.axis_size("grp")
    high, low = reduced_gram(matrix)
    scale = float((matrix.shape[0] * parts) ** 0.5)
    width = matrix.shape[1] // lax.axis_size("rows")
    basis, coeffs = finish((high.reshape(-1, 128), low.reshape(-1, 128), matrix, sketch), scale, width)
    return basis, coeffs.T


def solution(mesh):
    return jax.shard_map(
        shards,
        mesh=mesh,
        in_specs=(P(("rows", "grp"), None), P()),
        out_specs=(P(("rows", "grp"), None), P(None, "rows")),
        check_vma=False,
    )
```

```python
import functools
import jax
import jax.numpy as jnp
from jax import lax
from jax.experimental import pallas as pl
from jax.experimental.pallas import tpu as pltpu
from jax.sharding import PartitionSpec as P

MESH = pl.DeviceIdType.MESH
F32 = jnp.float32
BF16 = jnp.bfloat16
NX, NY, NZ = 4, 8, 8
BLOCKS = [(i, j) for i in range(6) for j in range(i, 6)]
LIVE = 336
HELD = 384
PIECE = 24


def split(v):
    high = v.astype(BF16)
    return high, (v - high.astype(F32)).astype(BF16)


NN = (((1,), (0,)), ((), ()))
NT = (((1,), (1,)), ((), ()))
TN = (((0,), (0,)), ((), ()))


def dot3(left, right, dims):
    def one(a, b):
        return lax.dot_general(a, b, dims, preferred_element_type=F32)
    return one(left[0], right[1]) + one(left[1], right[0]) + one(left[0], right[0])


def place(tile):
    share, row = divmod(tile, LIVE // 8)
    return share // NX, share % NX, row * 8


def store_block(part, index, value):
    for t in range(16):
        core, x, row = place(index * 16 + t)
        part[core, x, row:row + 8, :] = value[8 * t:8 * t + 8, :]


PARTS = (pl.ds(0, HELD // 2), pl.ds(HELD // 2, LIVE - HELD // 2))
SUBS = tuple((pl.ds(p.start, p.size // 2), pl.ds(p.start + p.size // 2, p.size // 2)) for p in PARTS)


def reduce_kernel(a_hbm, s_hbm, high, low, st_high, st_low, a_own, s_own, part, sib_in, relay_in, x_in, acc, z_in, y_in, zy, yz, gath, load_sem,
                  sib_s, sib_r, rl_s, rl_r, x_s, x_r, z_s, z_r, y_s, y_r, zy_s, zy_r, yz_s, yz_r,
                  zg_s, zg_r, yg_s, yg_r, xg_s, xg_r, fw_s, fw_r):
    r = lax.axis_index("rows")
    y = lax.axis_index("grp")
    x, z, c = r // 16, lax.rem(r // 2, 8), lax.rem(r, 2)

    def dev(xx, yy, zz, cc):
        return ((xx * NZ + zz) * 2 + cc, yy)

    def other(axis, k):
        if axis == "x":
            return lax.rem(x + k, NX), dev(lax.rem(x + k, NX), y, z, c)
        if axis == "y":
            return lax.rem(y + k, NY), dev(x, lax.rem(y + k, NY), z, c)
        return lax.rem(z + k, NZ), dev(x, y, lax.rem(z + k, NZ), c)

    sibling = dev(x, y, z, 1 - c)
    load = pltpu.make_async_copy(a_hbm, a_own, load_sem.at[0])
    load.start()
    barrier = pltpu.get_barrier_semaphore()
    for axis, n in (("x", NX), ("y", NY), ("z", NZ)):
        for k in range(1, n):
            pl.semaphore_signal(barrier, inc=1, device_id=other(axis, k)[1], device_id_type=MESH)
    pl.semaphore_signal(barrier, inc=1, device_id=sibling, device_id_type=MESH)
    load_s = pltpu.make_async_copy(s_hbm, s_own, load_sem.at[1])
    load_s.start()

    def copy(src, dst, s, rr, to=sibling):
        return pltpu.make_async_remote_copy(src_ref=src, dst_ref=dst, send_sem=s, recv_sem=rr,
                                            device_id=to, device_id_type=MESH)

    sent = []

    def send(*args):
        d = copy(*args)
        d.start()
        sent.append(d)

    load.wait()
    halves = split(a_own[...])
    for i in range(6):
        lo = 128 * i
        strip = dot3((halves[0][:, lo:lo + 128], halves[1][:, lo:lo + 128]), (halves[0][:, lo:], halves[1][:, lo:]), TN)
        for j in range(i, 6):
            store_block(part, BLOCKS.index((i, j)), strip[:, 128 * j - lo:128 * j - lo + 128])

    pl.semaphore_wait(barrier, 1 + (NX - 1) + (NY - 1) + (NZ - 1))

    right, to_right = other("x", 1)
    left, to_left = other("x", 3)
    across, _ = other("x", 2)
    for h, rows in enumerate(PARTS):
        for xx in (across, right, left, x):
            send(part.at[1 - c, xx, rows], sib_in.at[xx, rows], sib_s.at[h, xx], sib_r.at[h, xx], sibling)

    def add_sibling(h, xx):
        rows = PARTS[h]
        copy(part.at[1 - c, xx, rows], sib_in.at[xx, rows], sib_s.at[h, xx], sib_r.at[h, xx]).wait_recv()
        part[c, xx, rows, :] = part[c, xx, rows, :] + sib_in[xx, rows, :]

    def relay(h, n, to=sibling):
        rows = SUBS[h][n]
        return part.at[c, across, rows], relay_in.at[rows], rl_s.at[h, n], rl_r.at[h, n], to

    def one_step(h, way, n, to=sibling):
        rows = SUBS[h][n]
        return part.at[c, (right, left)[way], rows], x_in.at[way, rows], x_s.at[h, way, n], x_r.at[h, way, n], to

    for h in range(2):
        add_sibling(h, across)
        send(*relay(h, 0, to_right))
        send(*relay(h, 1, to_left))
        add_sibling(h, right)
        send(*one_step(h, 0, 1, to_right))
        add_sibling(h, left)
        send(*one_step(h, 1, 0, to_left))
        add_sibling(h, x)
    for h in range(2):
        for n, (xx, to) in enumerate(((right, to_right), (left, to_left))):
            rows = SUBS[h][n]
            copy(*relay(h, n)).wait_recv()
            part[c, xx, rows, :] = part[c, xx, rows, :] + relay_in[rows, :]
            send(*one_step(h, n, n, to))
    load_s.wait()
    st_high[...], st_low[...] = split(s_own[...].T)
    acc[LIVE:HELD, :] = jnp.zeros((HELD - LIVE, 128), F32)

    def piece(half, owner):
        return pl.ds(pl.multiple_of(half * (HELD // 2) + owner * PIECE, 8), PIECE)

    along = (("z", z, z_in, z_s, z_r), ("y", y, y_in, y_s, y_r))
    for h, (axis, me, box, ss, rs) in enumerate(along):
        rows = PARTS[h]
        for way, n in ((0, 1), (1, 0), (0, 0), (1, 1)):
            copy(*one_step(h, way, n)).wait_recv()
        acc[rows, :] = part[c, x, rows, :] + (x_in[0, rows, :] + x_in[1, rows, :])
        for k in (4, 3, 5, 2, 6, 1, 7):
            to, device = other(axis, k)
            send(acc.at[piece(h, to)], box.at[k - 1], ss.at[k - 1], rs.at[k - 1], device)
    cross = (("y", y, zy, zy_s, zy_r), ("z", z, yz, yz_s, yz_r))
    for h, (axis, me, box, ss, rs) in enumerate(along):
        for k in range(1, 8):
            copy(acc.at[piece(h, me)], box.at[k - 1], ss.at[k - 1], rs.at[k - 1]).wait_recv()
        total = acc[piece(h, me), :]
        for k in range(1, 8):
            total += box[k - 1]
        axis, me, box, ss, rs = cross[h]
        box[me] = total
        for k in (4, 3, 5, 2, 6, 1, 7):
            send(box.at[me], box.at[me], ss.at[k - 1], rs.at[me], other(axis, k)[1])
    mine = gath.at[c, x]
    back = (("z", z, zg_s, zg_r), ("y", y, yg_s, yg_r))
    for h, (axis, me, box, ss, rs) in enumerate(cross):
        for k in range(1, 8):
            at, _ = other(axis, k)
            copy(box.at[at], box.at[at], ss.at[k - 1], rs.at[at]).wait_recv()
        total = box[0]
        for k in range(1, 8):
            total += box[k]
        axis, me, ss, rs = back[h]
        gath[c, x, piece(h, me), :] = total
        for k in (4, 3, 5, 2, 6, 1, 7):
            send(mine.at[piece(h, me)], mine.at[piece(h, me)], ss.at[k - 1], rs.at[me], other(axis, k)[1])
    def halve(core, xx, h):
        share = core * NX + xx
        for n in range(PARTS[h].size // 16):
            row = PARTS[h].start + 16 * n
            high[share, row:row + 16, :], low[share, row:row + 16, :] = split(gath[core, xx, row:row + 16, :])

    def whole(h, xx):
        ref = gath.at[c, xx, PARTS[h]]
        return ref, ref, fw_s.at[h, xx], fw_r.at[h, xx], sibling

    for h, (axis, me, ss, rs) in enumerate(back):
        for k in range(1, 8):
            at, _ = other(axis, k)
            copy(mine.at[piece(h, at)], mine.at[piece(h, at)], ss.at[k - 1], rs.at[at]).wait_recv()
        rows = PARTS[h]
        for k in (2, 1, 3):
            send(mine.at[rows], mine.at[rows], xg_s.at[h, k - 1], xg_r.at[h, x], other("x", k)[1])
        send(*whole(h, x))
        halve(c, x, h)
    for h, rows in enumerate(PARTS):
        for xx in (left, right, across):
            came = gath.at[c, xx, rows]
            copy(came, came, xg_s.at[h, 0], xg_r.at[h, xx]).wait_recv()
            send(*whole(h, xx))
            halve(c, xx, h)
    for h, rows in enumerate(PARTS):
        for xx in (x, left, right, across):
            came = gath.at[1 - c, xx, rows]
            copy(came, came, fw_s.at[h, xx], fw_r.at[h, xx]).wait_recv()
            halve(1 - c, xx, h)
    for d in sent:
        d.wait_send()


def dma(*shape):
    return pltpu.SemaphoreType.DMA(shape)


def reduced_gram(matrix, sketch):
    rows, cols = matrix.shape
    vmem = pl.BlockSpec(memory_space=pltpu.VMEM)
    return pl.pallas_call(
        reduce_kernel,
        out_shape=[jax.ShapeDtypeStruct((2 * NX, LIVE, 128), BF16)] * 2 + [jax.ShapeDtypeStruct(sketch.shape[::-1], BF16)] * 2,
        in_specs=[pl.BlockSpec(memory_space=pltpu.HBM)] * 2,
        out_specs=[vmem] * 4,
        scratch_shapes=[
            pltpu.VMEM((rows, cols), F32),
            pltpu.VMEM(sketch.shape, F32),
            pltpu.VMEM((2, NX, HELD, 128), F32),
            pltpu.VMEM((NX, LIVE, 128), F32),
            pltpu.VMEM((LIVE, 128), F32),
            pltpu.VMEM((2, LIVE, 128), F32),
            pltpu.VMEM((HELD, 128), F32),
            pltpu.VMEM((7, PIECE, 128), F32),
            pltpu.VMEM((7, PIECE, 128), F32),
            pltpu.VMEM((8, PIECE, 128), F32),
            pltpu.VMEM((8, PIECE, 128), F32),
            pltpu.VMEM((2, NX, HELD, 128), F32),
            dma(2),
            dma(2, 4), dma(2, 4), dma(2, 2), dma(2, 2), dma(2, 2, 2), dma(2, 2, 2), dma(7), dma(7), dma(7), dma(7),
            dma(7), dma(8), dma(7), dma(8), dma(7), dma(8), dma(7), dma(8),
            dma(2, 3), dma(2, 4), dma(2, 4), dma(2, 4),
        ],
        compiler_params=pltpu.CompilerParams(collective_id=0, has_side_effects=True,
                                             vmem_limit_bytes=103 * 512 * 1024),
        name="reduce_gram",
    )(matrix, sketch)


NB = 64


def spread(v):
    return jnp.broadcast_to(v, (8, 128))


def eliminate(w, at):
    n8 = w.shape[0] // 8
    lanes = range(w.shape[1] // 128)
    groups = [[w[8 * g:8 * g + 8, 128 * v:128 * v + 128] for v in lanes] for g in range(n8)]
    sub = lax.broadcasted_iota(jnp.int32, (8, 128), 0)
    out = []
    for g in range(n8):
        base = at + 8 * g
        cols = {h: [spread(groups[h][0][:, base + k:base + k + 1]) for k in range(8)] for h in range(g, n8)}
        pairs = []
        for k in range(0, 8, 2):
            e0 = {m: spread(cols[g][m][k:k + 1, :]) for m in range(k, 8)}
            e1 = {m: spread(cols[g][m][k + 1:k + 2, :]) for m in range(k + 1, 8)}
            a, b, c = e0[k], e0[k + 1], e1[k + 1]
            det = a * c - b * b
            inv = 1.0 / det
            pairs.append((a, b, det))
            v0 = {m: (c * e0[m] - b * e1[m]) * inv for m in range(k + 2, 8)}
            v1 = {m: (a * e1[m] - b * e0[m]) * inv for m in range(k + 2, 8)}
            u = []
            for v in lanes:
                r0, r1 = spread(groups[g][v][k:k + 1, :]), spread(groups[g][v][k + 1:k + 2, :])
                u.append(((c * r0 - b * r1) * inv, (a * r1 - b * r0) * inv))
            for h in range(g, n8):
                c0, c1 = cols[h][k], cols[h][k + 1]
                if h == g:
                    if k == 6:
                        continue
                    c0, c1 = jnp.where(sub > k + 1, c0, 0.0), jnp.where(sub > k + 1, c1, 0.0)
                for m in range(k + 2, 8):
                    cols[h][m] = cols[h][m] - (c0 * v0[m] + c1 * v1[m])
                for v in lanes:
                    groups[h][v] = groups[h][v] - (c0 * u[v][0] + c1 * u[v][1])
        less, scale = jnp.zeros((8, 128), F32), jnp.zeros((8, 128), F32)
        for i, (a, b, det) in enumerate(pairs):
            root = lax.rsqrt(a)
            less = jnp.where(sub == 2 * i + 1, b / a, less)
            scale = jnp.where(sub == 2 * i, root, jnp.where(sub == 2 * i + 1, a * root * lax.rsqrt(det), scale))
        out.append(jnp.concatenate([(p - less * pltpu.roll(p, 1, 0)) * scale for p in groups[g]], 1))
    return jnp.concatenate(out, 0)


def cholesky_inverse(gram, linv, work):
    n, nb = gram.shape[0], NB
    same = lax.broadcasted_iota(jnp.int32, (n, n), 0) == lax.broadcasted_iota(jnp.int32, (n, n), 1)
    diagonal = jnp.where(same, gram, 0.0)
    unit = lax.rsqrt(jnp.sum(diagonal, 0, keepdims=True))
    work[:, 0:n] = gram * unit * lax.rsqrt(jnp.sum(diagonal, 1, keepdims=True))
    work[:, n:] = jnp.where(same, 1.0, 0.0)
    linv[...] = jnp.zeros((n, n), F32)
    for lo in range(0, n, nb):
        hi = lo + nb
        first, last = lo // 128 * 128, -(-hi // 128) * 128
        rows = eliminate(jnp.concatenate([work[lo:hi, first:n], work[lo:hi, n:n + last]], 1), lo - first)
        linv[lo:hi, 0:last] = rows[:, n - first:] * unit[:, 0:last]
        if hi < n:
            begin = hi // 128 * 128
            halves = split(rows)
            left = tuple(v[:, begin - first:n - first] for v in halves)
            if begin > first:
                halves = tuple(v[:, begin - first:] for v in halves)
            less = dot3(left, halves, TN)[hi - begin:, :]
            work[hi:n, begin:n] = work[hi:n, begin:n] - less[:, 0:n - begin]
            work[hi:n, n:n + last] = work[hi:n, n:n + last] - less[:, n - begin:]


def upper(ref, i, j):
    at = 128 * BLOCKS.index((i, j))
    return ref[at:at + 128, :]


def gram_strips(ref, corners):
    strips = []
    for s in range(3):
        p, q = 2 * s, 2 * s + 1
        above = [jnp.concatenate([upper(ref, i, p), upper(ref, i, q)], 1) for i in range(q)]
        above.append(jnp.concatenate([corners[s], upper(ref, q, q)], 1))
        right = None
        if s < 2:
            right = jnp.concatenate([jnp.concatenate([upper(ref, i, j) for j in range(q + 1, 6)], 1) for i in (p, q)], 0)
        strips.append((jnp.concatenate(above, 0), right))
    return strips


def times_gram(left, high, low):
    out = []
    for s in range(3):
        hi = 256 * s + 256
        strip = dot3((left[0][:, :hi], left[1][:, :hi]), (high[s][0], low[s][0]), NN)
        if s < 2:
            strip += dot3((left[0][:, hi:], left[1][:, hi:]), (high[s][1], low[s][1]), NT)
        out.append(strip)
    return jnp.concatenate(out, 1)


def finish_kernel(scale, g_high, g_low, st_high, st_low, a_hbm, basis_ref, coeffs_ref, work, linv, a_own, load_sem):
    load = pltpu.make_async_copy(a_hbm, a_own, load_sem)
    load.start()
    r = lax.axis_index("rows")
    high, low = (gram_strips(ref, [upper(ref, 2 * s, 2 * s + 1).T for s in range(3)]) for ref in (g_high, g_low))
    power = split(times_gram((st_high[...], st_low[...]), high, low))
    ranged = times_gram(power, high, low)
    halves = split(ranged)
    cholesky_inverse(dot3(halves, power, NT), linv, work)
    inverse = split(linv[...])
    factor = split(dot3(inverse, power, NN))
    load.wait()
    basis_ref[...] = dot3(split(a_own[...]), factor, NT) * scale
    width = coeffs_ref.shape[0]
    row = lax.broadcasted_iota(jnp.int32, (128, 768), 0)
    col = lax.broadcasted_iota(jnp.int32, (128, 768), 1)
    pick = jnp.where(col == row + r * width, 1.0, 0.0).astype(BF16)
    rest = (ranged - halves[0].astype(F32)) - halves[1].astype(F32)
    mine = sum(lax.dot_general(pick, part, NT, preferred_element_type=F32)
               for part in (halves[0], halves[1], rest.astype(BF16)))
    coeffs_ref[...] = dot3(split(mine), inverse, NT)[0:width, :]


def finish(operands, scale, width):
    vmem = pl.BlockSpec(memory_space=pltpu.VMEM)
    return pl.pallas_call(
        functools.partial(finish_kernel, scale),
        out_shape=(jax.ShapeDtypeStruct((256, 256), F32), jax.ShapeDtypeStruct((width, 256), F32)),
        in_specs=[vmem] * 4 + [pl.BlockSpec(memory_space=pltpu.HBM)],
        out_specs=(vmem, vmem),
        scratch_shapes=[
            pltpu.VMEM((256, 512), F32),
            pltpu.VMEM((256, 256), F32),
            pltpu.VMEM((256, 768), F32),
            pltpu.SemaphoreType.DMA,
        ],
        compiler_params=pltpu.CompilerParams(vmem_limit_bytes=40 * 1024 * 1024),
        name="finish",
    )(*operands)


def shards(matrix, sketch):
    parts = lax.axis_size("rows") * lax.axis_size("grp")
    high, low, *rest = reduced_gram(matrix, sketch)
    scale = float((matrix.shape[0] * parts) ** 0.5)
    width = matrix.shape[1] // lax.axis_size("rows")
    basis, coeffs = finish((high.reshape(-1, 128), low.reshape(-1, 128), *rest, matrix), scale, width)
    return basis, coeffs.T


def solution(mesh):
    return jax.shard_map(
        shards,
        mesh=mesh,
        in_specs=(P(("rows", "grp"), None), P()),
        out_specs=(P(("rows", "grp"), None), P(None, "rows")),
        check_vma=False,
    )
```

```python
import functools
import jax
import jax.numpy as jnp
from jax import lax
from jax.experimental import pallas as pl
from jax.experimental.pallas import tpu as pltpu
from jax.sharding import PartitionSpec as P

MESH = pl.DeviceIdType.MESH
F32 = jnp.float32
BF16 = jnp.bfloat16
NX, NY, NZ = 4, 8, 8
BLOCKS = [(i, j) for i in range(6) for j in range(i, 6)]
LIVE = 336
HELD = 384
PIECE = 24


def split(v):
    high = v.astype(BF16)
    return high, (v - high.astype(F32)).astype(BF16)


NN = (((1,), (0,)), ((), ()))
NT = (((1,), (1,)), ((), ()))
TN = (((0,), (0,)), ((), ()))


def dot3(left, right, dims):
    def one(a, b):
        return lax.dot_general(a, b, dims, preferred_element_type=F32)
    return one(left[0], right[1]) + one(left[1], right[0]) + one(left[0], right[0])


def place(tile):
    share, row = divmod(tile, LIVE // 8)
    return share // NX, share % NX, row * 8


def store_block(part, index, value):
    for t in range(16):
        core, x, row = place(index * 16 + t)
        part[core, x, row:row + 8, :] = value[8 * t:8 * t + 8, :]


PARTS = (pl.ds(0, HELD // 2), pl.ds(HELD // 2, LIVE - HELD // 2))
SUBS = tuple((pl.ds(p.start, p.size // 2), pl.ds(p.start + p.size // 2, p.size // 2)) for p in PARTS)


def reduce_kernel(a_hbm, s_hbm, high, low, st_high, st_low, a_own, s_own, part, sib_in, relay_in, x_in, acc, z_in, y_in, zy, yz, gath, load_sem,
                  sib_s, sib_r, rl_s, rl_r, x_s, x_r, z_s, z_r, y_s, y_r, zy_s, zy_r, yz_s, yz_r,
                  zg_s, zg_r, yg_s, yg_r, xg_s, xg_r, fw_s, fw_r):
    r = lax.axis_index("rows")
    y = lax.axis_index("grp")
    x, z, c = r // 16, lax.rem(r // 2, 8), lax.rem(r, 2)

    def dev(xx, yy, zz, cc):
        return ((xx * NZ + zz) * 2 + cc, yy)

    def other(axis, k):
        if axis == "x":
            return lax.rem(x + k, NX), dev(lax.rem(x + k, NX), y, z, c)
        if axis == "y":
            return lax.rem(y + k, NY), dev(x, lax.rem(y + k, NY), z, c)
        return lax.rem(z + k, NZ), dev(x, y, lax.rem(z + k, NZ), c)

    sibling = dev(x, y, z, 1 - c)
    load = pltpu.make_async_copy(a_hbm, a_own, load_sem.at[0])
    load.start()
    barrier = pltpu.get_barrier_semaphore()
    for axis, n in (("x", NX), ("y", NY), ("z", NZ)):
        for k in range(1, n):
            pl.semaphore_signal(barrier, inc=1, device_id=other(axis, k)[1], device_id_type=MESH)
    pl.semaphore_signal(barrier, inc=1, device_id=sibling, device_id_type=MESH)
    load_s = pltpu.make_async_copy(s_hbm, s_own, load_sem.at[1])
    load_s.start()

    def copy(src, dst, s, rr, to=sibling):
        return pltpu.make_async_remote_copy(src_ref=src, dst_ref=dst, send_sem=s, recv_sem=rr,
                                            device_id=to, device_id_type=MESH)

    sent = []

    def send(*args):
        d = copy(*args)
        d.start()
        sent.append(d)

    load.wait()
    halves = split(a_own[...])
    for i in range(6):
        lo = 128 * i
        strip = dot3((halves[0][:, lo:lo + 128], halves[1][:, lo:lo + 128]), (halves[0][:, lo:], halves[1][:, lo:]), TN)
        for j in range(i, 6):
            store_block(part, BLOCKS.index((i, j)), strip[:, 128 * j - lo:128 * j - lo + 128])

    pl.semaphore_wait(barrier, 1 + (NX - 1) + (NY - 1) + (NZ - 1))

    right, to_right = other("x", 1)
    left, to_left = other("x", 3)
    across, _ = other("x", 2)
    for h, xx in [(h, xx) for group in ((across,), (right, left), (x,)) for h in range(2) for xx in group]:
        rows = PARTS[h]
        send(part.at[1 - c, xx, rows], sib_in.at[xx, rows], sib_s.at[h, xx], sib_r.at[h, xx], sibling)

    def add_sibling(h, xx):
        rows = PARTS[h]
        copy(part.at[1 - c, xx, rows], sib_in.at[xx, rows], sib_s.at[h, xx], sib_r.at[h, xx]).wait_recv()
        part[c, xx, rows, :] = part[c, xx, rows, :] + sib_in[xx, rows, :]

    def relay(h, n, to=sibling):
        rows = SUBS[h][n]
        return part.at[c, across, rows], relay_in.at[rows], rl_s.at[h, n], rl_r.at[h, n], to

    def one_step(h, way, n, to=sibling):
        rows = SUBS[h][n]
        return part.at[c, (right, left)[way], rows], x_in.at[way, rows], x_s.at[h, way, n], x_r.at[h, way, n], to

    for h in range(2):
        add_sibling(h, across)
        send(*relay(h, 0, to_right))
        send(*relay(h, 1, to_left))
    for h in range(2):
        add_sibling(h, right)
        send(*one_step(h, 0, 1, to_right))
        add_sibling(h, left)
        send(*one_step(h, 1, 0, to_left))
    for h in range(2):
        add_sibling(h, x)
    for h in range(2):
        for n, (xx, to) in enumerate(((right, to_right), (left, to_left))):
            rows = SUBS[h][n]
            copy(*relay(h, n)).wait_recv()
            part[c, xx, rows, :] = part[c, xx, rows, :] + relay_in[rows, :]
            send(*one_step(h, n, n, to))
    load_s.wait()
    st_high[...], st_low[...] = split(s_own[...].T)
    acc[LIVE:HELD, :] = jnp.zeros((HELD - LIVE, 128), F32)

    def piece(half, owner):
        return pl.ds(pl.multiple_of(half * (HELD // 2) + owner * PIECE, 8), PIECE)

    along = (("z", z, z_in, z_s, z_r), ("y", y, y_in, y_s, y_r))
    for h, (axis, me, box, ss, rs) in enumerate(along):
        rows = PARTS[h]
        for way, n in ((0, 1), (1, 0), (0, 0), (1, 1)):
            copy(*one_step(h, way, n)).wait_recv()
        acc[rows, :] = part[c, x, rows, :] + (x_in[0, rows, :] + x_in[1, rows, :])
        for k in (4, 3, 5, 2, 6, 1, 7):
            to, device = other(axis, k)
            send(acc.at[piece(h, to)], box.at[k - 1], ss.at[k - 1], rs.at[k - 1], device)
    cross = (("y", y, zy, zy_s, zy_r), ("z", z, yz, yz_s, yz_r))
    for h, (axis, me, box, ss, rs) in enumerate(along):
        for k in range(1, 8):
            copy(acc.at[piece(h, me)], box.at[k - 1], ss.at[k - 1], rs.at[k - 1]).wait_recv()
        total = acc[piece(h, me), :]
        for k in range(1, 8):
            total += box[k - 1]
        axis, me, box, ss, rs = cross[h]
        box[me] = total
        for k in (4, 3, 5, 2, 6, 1, 7):
            send(box.at[me], box.at[me], ss.at[k - 1], rs.at[me], other(axis, k)[1])
    mine = gath.at[c, x]
    back = (("z", z, zg_s, zg_r), ("y", y, yg_s, yg_r))
    for h, (axis, me, box, ss, rs) in enumerate(cross):
        for k in range(1, 8):
            at, _ = other(axis, k)
            copy(box.at[at], box.at[at], ss.at[k - 1], rs.at[at]).wait_recv()
        total = box[0]
        for k in range(1, 8):
            total += box[k]
        axis, me, ss, rs = back[h]
        gath[c, x, piece(h, me), :] = total
        for k in (4, 3, 5, 2, 6, 1, 7):
            send(mine.at[piece(h, me)], mine.at[piece(h, me)], ss.at[k - 1], rs.at[me], other(axis, k)[1])
    def halve(core, xx, h):
        share = core * NX + xx
        for n in range(PARTS[h].size // 16):
            row = PARTS[h].start + 16 * n
            high[share, row:row + 16, :], low[share, row:row + 16, :] = split(gath[core, xx, row:row + 16, :])

    def whole(h, xx):
        ref = gath.at[c, xx, PARTS[h]]
        return ref, ref, fw_s.at[h, xx], fw_r.at[h, xx], sibling

    for h, (axis, me, ss, rs) in enumerate(back):
        for k in range(1, 8):
            at, _ = other(axis, k)
            copy(mine.at[piece(h, at)], mine.at[piece(h, at)], ss.at[k - 1], rs.at[at]).wait_recv()
        rows = PARTS[h]
        for k in (2, 1, 3):
            send(mine.at[rows], mine.at[rows], xg_s.at[h, k - 1], xg_r.at[h, x], other("x", k)[1])
        send(*whole(h, x))
        halve(c, x, h)
    for h, rows in enumerate(PARTS):
        for xx in (left, right, across):
            came = gath.at[c, xx, rows]
            copy(came, came, xg_s.at[h, 0], xg_r.at[h, xx]).wait_recv()
            send(*whole(h, xx))
            halve(c, xx, h)
    for h, rows in enumerate(PARTS):
        for xx in (x, left, right, across):
            came = gath.at[1 - c, xx, rows]
            copy(came, came, fw_s.at[h, xx], fw_r.at[h, xx]).wait_recv()
            halve(1 - c, xx, h)
    for d in sent:
        d.wait_send()


def dma(*shape):
    return pltpu.SemaphoreType.DMA(shape)


def reduced_gram(matrix, sketch):
    rows, cols = matrix.shape
    vmem = pl.BlockSpec(memory_space=pltpu.VMEM)
    return pl.pallas_call(
        reduce_kernel,
        out_shape=[jax.ShapeDtypeStruct((2 * NX, LIVE, 128), BF16)] * 2 + [jax.ShapeDtypeStruct(sketch.shape[::-1], BF16)] * 2,
        in_specs=[pl.BlockSpec(memory_space=pltpu.HBM)] * 2,
        out_specs=[vmem] * 4,
        scratch_shapes=[
            pltpu.VMEM((rows, cols), F32),
            pltpu.VMEM(sketch.shape, F32),
            pltpu.VMEM((2, NX, HELD, 128), F32),
            pltpu.VMEM((NX, LIVE, 128), F32),
            pltpu.VMEM((LIVE, 128), F32),
            pltpu.VMEM((2, LIVE, 128), F32),
            pltpu.VMEM((HELD, 128), F32),
            pltpu.VMEM((7, PIECE, 128), F32),
            pltpu.VMEM((7, PIECE, 128), F32),
            pltpu.VMEM((8, PIECE, 128), F32),
            pltpu.VMEM((8, PIECE, 128), F32),
            pltpu.VMEM((2, NX, HELD, 128), F32),
            dma(2),
            dma(2, 4), dma(2, 4), dma(2, 2), dma(2, 2), dma(2, 2, 2), dma(2, 2, 2), dma(7), dma(7), dma(7), dma(7),
            dma(7), dma(8), dma(7), dma(8), dma(7), dma(8), dma(7), dma(8),
            dma(2, 3), dma(2, 4), dma(2, 4), dma(2, 4),
        ],
        compiler_params=pltpu.CompilerParams(collective_id=0, has_side_effects=True,
                                             vmem_limit_bytes=103 * 512 * 1024),
        name="reduce_gram",
    )(matrix, sketch)


def spread(v):
    return jnp.broadcast_to(v, (8, 128))


def eliminate(w, at):
    n8 = w.shape[0] // 8
    lanes = range(w.shape[1] // 128)
    groups = [[w[8 * g:8 * g + 8, 128 * v:128 * v + 128] for v in lanes] for g in range(n8)]
    sub = lax.broadcasted_iota(jnp.int32, (8, 128), 0)
    out = []
    for g in range(n8):
        base = at + 8 * g
        cols = {h: [spread(groups[h][0][:, base + k:base + k + 1]) for k in range(8)] for h in range(g, n8)}
        pairs = []
        for k in range(0, 8, 2):
            e0 = {m: spread(cols[g][m][k:k + 1, :]) for m in range(k, 8)}
            e1 = {m: spread(cols[g][m][k + 1:k + 2, :]) for m in range(k + 1, 8)}
            a, b, c = e0[k], e0[k + 1], e1[k + 1]
            det = a * c - b * b
            inv = 1.0 / det
            pairs.append((a, b, det))
            v0 = {m: (c * e0[m] - b * e1[m]) * inv for m in range(k + 2, 8)}
            v1 = {m: (a * e1[m] - b * e0[m]) * inv for m in range(k + 2, 8)}
            u = []
            for v in lanes:
                r0, r1 = spread(groups[g][v][k:k + 1, :]), spread(groups[g][v][k + 1:k + 2, :])
                u.append(((c * r0 - b * r1) * inv, (a * r1 - b * r0) * inv))
            for h in range(g, n8):
                c0, c1 = cols[h][k], cols[h][k + 1]
                if h == g:
                    if k == 6:
                        continue
                    c0, c1 = jnp.where(sub > k + 1, c0, 0.0), jnp.where(sub > k + 1, c1, 0.0)
                for m in range(k + 2, 8):
                    cols[h][m] = cols[h][m] - (c0 * v0[m] + c1 * v1[m])
                for v in lanes:
                    groups[h][v] = groups[h][v] - (c0 * u[v][0] + c1 * u[v][1])
        less, scale = jnp.zeros((8, 128), F32), jnp.zeros((8, 128), F32)
        for i, (a, b, det) in enumerate(pairs):
            root = lax.rsqrt(a)
            less = jnp.where(sub == 2 * i + 1, b / a, less)
            scale = jnp.where(sub == 2 * i, root, jnp.where(sub == 2 * i + 1, a * root * lax.rsqrt(det), scale))
        out.append(jnp.concatenate([(p - less * pltpu.roll(p, 1, 0)) * scale for p in groups[g]], 1))
    return jnp.concatenate(out, 0)


def cholesky_inverse(gram, work, use):
    n, nb = gram.shape[0], 64
    same = lax.broadcasted_iota(jnp.int32, (n, n), 0) == lax.broadcasted_iota(jnp.int32, (n, n), 1)
    diagonal = jnp.where(same, gram, 0.0)
    unit = lax.rsqrt(jnp.sum(diagonal, 0, keepdims=True))
    work[:, 0:n] = gram * unit * lax.rsqrt(jnp.sum(diagonal, 1, keepdims=True))
    work[:, n:] = jnp.where(same, 1.0, 0.0)
    for lo in range(0, n, nb):
        hi = lo + nb
        first, last = lo // 128 * 128, -(-hi // 128) * 128
        rows = eliminate(jnp.concatenate([work[lo:hi, first:n], work[lo:hi, n:n + last]], 1), lo - first)
        if hi < n:
            begin = hi // 128 * 128
            halves = split(rows)
            if begin > first:
                halves = tuple(v[:, begin - first:] for v in halves)
            for top in (hi,) if hi + nb == n else (hi, hi + nb):
                end = hi + nb if top == hi else n
                left = tuple(v[:, top - begin:end - begin] for v in halves)
                less = dot3(left, halves, TN)
                work[top:end, begin:n] = work[top:end, begin:n] - less[:, 0:n - begin]
                work[top:end, n:n + last] = work[top:end, n:n + last] - less[:, n - begin:]
        use(lo, rows[:, n - first:] * unit[:, 0:last])


def upper(ref, i, j):
    at = 128 * BLOCKS.index((i, j))
    return ref[at:at + 128, :]


def gram_strips(ref, corners):
    strips = []
    for s in range(3):
        p, q = 2 * s, 2 * s + 1
        above = [jnp.concatenate([upper(ref, i, p), upper(ref, i, q)], 1) for i in range(q)]
        above.append(jnp.concatenate([corners[s], upper(ref, q, q)], 1))
        right = None
        if s < 2:
            right = jnp.concatenate([jnp.concatenate([upper(ref, i, j) for j in range(q + 1, 6)], 1) for i in (p, q)], 0)
        strips.append((jnp.concatenate(above, 0), right))
    return strips


def times_gram(left, high, low):
    out = []
    for s in range(3):
        hi = 256 * s + 256
        strip = dot3((left[0][:, :hi], left[1][:, :hi]), (high[s][0], low[s][0]), NN)
        if s < 2:
            strip += dot3((left[0][:, hi:], left[1][:, hi:]), (high[s][1], low[s][1]), NT)
        out.append(strip)
    return jnp.concatenate(out, 1)


def finish_kernel(scale, g_high, g_low, st_high, st_low, a_hbm, basis_ref, coeffs_ref, work, a_own, load_sem):
    load = pltpu.make_async_copy(a_hbm, a_own, load_sem)
    load.start()
    r = lax.axis_index("rows")
    high, low = (gram_strips(ref, [upper(ref, 2 * s, 2 * s + 1).T for s in range(3)]) for ref in (g_high, g_low))
    power = split(times_gram((st_high[...], st_low[...]), high, low))
    ranged = times_gram(power, high, low)
    halves = split(ranged)
    gram = dot3(halves, power, NT)
    width = coeffs_ref.shape[0]
    row = lax.broadcasted_iota(jnp.int32, (128, 768), 0)
    col = lax.broadcasted_iota(jnp.int32, (128, 768), 1)
    pick = jnp.where(col == row + r * width, 1.0, 0.0).astype(BF16)
    rest = (ranged - halves[0].astype(F32)) - halves[1].astype(F32)
    mine = split(sum(lax.dot_general(pick, part, NT, preferred_element_type=F32)
                     for part in (halves[0], halves[1], rest.astype(BF16))))
    load.wait()
    range_rows = split(dot3(split(a_own[...]), power, NT) * scale)

    def use(lo, rows):
        nb, last = rows.shape
        factor = split(rows)
        for out, left in ((basis_ref, range_rows), (coeffs_ref, mine)):
            value = dot3((left[0][:, 0:last], left[1][:, 0:last]), factor, NT)
            out[:, lo:lo + nb] = value[0:out.shape[0], :]

    cholesky_inverse(gram, work, use)


def finish(operands, scale, width):
    vmem = pl.BlockSpec(memory_space=pltpu.VMEM)
    return pl.pallas_call(
        functools.partial(finish_kernel, scale),
        out_shape=(jax.ShapeDtypeStruct((256, 256), F32), jax.ShapeDtypeStruct((width, 256), F32)),
        in_specs=[vmem] * 4 + [pl.BlockSpec(memory_space=pltpu.HBM)],
        out_specs=(vmem, vmem),
        scratch_shapes=[
            pltpu.VMEM((256, 512), F32),
            pltpu.VMEM((256, 768), F32),
            pltpu.SemaphoreType.DMA,
        ],
        compiler_params=pltpu.CompilerParams(vmem_limit_bytes=40 * 1024 * 1024),
        name="finish",
    )(*operands)


def shards(matrix, sketch):
    parts = lax.axis_size("rows") * lax.axis_size("grp")
    high, low, *rest = reduced_gram(matrix, sketch)
    scale = float((matrix.shape[0] * parts) ** 0.5)
    width = matrix.shape[1] // lax.axis_size("rows")
    basis, coeffs = finish((high.reshape(-1, 128), low.reshape(-1, 128), *rest, matrix), scale, width)
    return basis, coeffs.T


def solution(mesh):
    return jax.shard_map(
        shards,
        mesh=mesh,
        in_specs=(P(("rows", "grp"), None), P()),
        out_specs=(P(("rows", "grp"), None), P(None, "rows")),
        check_vma=False,
    )
```

```python
import functools
import jax
import jax.numpy as jnp
from jax import lax
from jax.experimental import pallas as pl
from jax.experimental.pallas import tpu as pltpu
from jax.sharding import PartitionSpec as P

MESH = pl.DeviceIdType.MESH
F32 = jnp.float32
BF16 = jnp.bfloat16
NX, NY, NZ = 4, 8, 8
BLOCKS = [(i, j) for i in range(6) for j in range(i, 6)]
LIVE = 336
HELD = 384
PIECE = 24


def split(v):
    high = v.astype(BF16)
    return high, (v - high.astype(F32)).astype(BF16)


NN = (((1,), (0,)), ((), ()))
NT = (((1,), (1,)), ((), ()))
TN = (((0,), (0,)), ((), ()))


def dot3(left, right, dims):
    def one(a, b):
        return lax.dot_general(a, b, dims, preferred_element_type=F32)
    return one(left[0], right[1]) + one(left[1], right[0]) + one(left[0], right[0])


def place(tile):
    share, row = divmod(tile, LIVE // 8)
    return share // NX, share % NX, row * 8


def store_block(part, index, value):
    for t in range(16):
        core, x, row = place(index * 16 + t)
        part[core, x, row:row + 8, :] = value[8 * t:8 * t + 8, :]


PARTS = (pl.ds(0, HELD // 2), pl.ds(HELD // 2, LIVE - HELD // 2))
SUBS = tuple((pl.ds(p.start, p.size // 2), pl.ds(p.start + p.size // 2, p.size // 2)) for p in PARTS)


def reduce_kernel(a_hbm, s_hbm, high, low, st_high, st_low, a_own, s_own, part, sib_in, relay_in, x_in, acc, z_in, y_in, zy, yz, gath, hand, load_sem,
                  sib_s, sib_r, rl_s, rl_r, x_s, x_r, z_s, z_r, y_s, y_r, zy_s, zy_r, yz_s, yz_r,
                  zg_s, zg_r, yg_s, yg_r, xg_s, xg_r, fw_s, fw_r):
    r = lax.axis_index("rows")
    y = lax.axis_index("grp")
    x, z, c = r // 16, lax.rem(r // 2, 8), lax.rem(r, 2)

    def dev(xx, yy, zz, cc):
        return ((xx * NZ + zz) * 2 + cc, yy)

    def other(axis, k):
        if axis == "x":
            return lax.rem(x + k, NX), dev(lax.rem(x + k, NX), y, z, c)
        if axis == "y":
            return lax.rem(y + k, NY), dev(x, lax.rem(y + k, NY), z, c)
        return lax.rem(z + k, NZ), dev(x, y, lax.rem(z + k, NZ), c)

    sibling = dev(x, y, z, 1 - c)
    load = pltpu.make_async_copy(a_hbm, a_own, load_sem.at[0])
    load.start()
    barrier = pltpu.get_barrier_semaphore()

    @pl.when(c == 1)
    def _():
        pl.semaphore_signal(barrier, inc=1, device_id=sibling, device_id_type=MESH)

    @pl.when(c == 0)
    def _():
        pl.semaphore_wait(barrier, 1)
        pl.semaphore_signal(hand, inc=1, device_id=sibling, device_id_type=MESH)

    @pl.when(c == 1)
    def _():
        pl.semaphore_wait(hand, 1)
        for axis, n in (("x", NX), ("y", NY), ("z", NZ)):
            for k in range(1, n):
                pl.semaphore_signal(barrier, inc=1, device_id=other(axis, k)[1], device_id_type=MESH)

    load_s = pltpu.make_async_copy(s_hbm, s_own, load_sem.at[1])
    load_s.start()

    def copy(src, dst, s, rr, to=sibling):
        return pltpu.make_async_remote_copy(src_ref=src, dst_ref=dst, send_sem=s, recv_sem=rr,
                                            device_id=to, device_id_type=MESH)

    sent = []

    def send(*args):
        d = copy(*args)
        d.start()
        sent.append(d)

    load.wait()
    halves = split(a_own[...])
    for i in range(6):
        lo = 128 * i
        strip = dot3((halves[0][:, lo:lo + 128], halves[1][:, lo:lo + 128]), (halves[0][:, lo:], halves[1][:, lo:]), TN)
        for j in range(i, 6):
            store_block(part, BLOCKS.index((i, j)), strip[:, 128 * j - lo:128 * j - lo + 128])

    right, to_right = other("x", 1)
    left, to_left = other("x", 3)
    across, _ = other("x", 2)
    for h, xx in [(h, xx) for group in ((across,), (right, left), (x,)) for h in range(2) for xx in group]:
        rows = PARTS[h]
        send(part.at[1 - c, xx, rows], sib_in.at[xx, rows], sib_s.at[h, xx], sib_r.at[h, xx], sibling)

    def add_sibling(h, xx):
        rows = PARTS[h]
        copy(part.at[1 - c, xx, rows], sib_in.at[xx, rows], sib_s.at[h, xx], sib_r.at[h, xx]).wait_recv()
        part[c, xx, rows, :] = part[c, xx, rows, :] + sib_in[xx, rows, :]

    def relay(h, n, to=sibling):
        rows = SUBS[h][n]
        return part.at[c, across, rows], relay_in.at[rows], rl_s.at[h, n], rl_r.at[h, n], to

    def one_step(h, way, n, to=sibling):
        rows = SUBS[h][n]
        return part.at[c, (right, left)[way], rows], x_in.at[way, rows], x_s.at[h, way, n], x_r.at[h, way, n], to

    @pl.when(c == 1)
    def _():
        pl.semaphore_wait(barrier, (NX - 1) + (NY - 1) + (NZ - 1))
        pl.semaphore_signal(hand, inc=1, device_id=sibling, device_id_type=MESH)

    @pl.when(c == 0)
    def _():
        pl.semaphore_wait(hand, 1)

    for h in range(2):
        add_sibling(h, across)
        send(*relay(h, 0, to_right))
        send(*relay(h, 1, to_left))
    for h in range(2):
        add_sibling(h, right)
        send(*one_step(h, 0, 1, to_right))
        add_sibling(h, left)
        send(*one_step(h, 1, 0, to_left))
    for h in range(2):
        add_sibling(h, x)
    for h in range(2):
        for n, (xx, to) in enumerate(((right, to_right), (left, to_left))):
            rows = SUBS[h][n]
            copy(*relay(h, n)).wait_recv()
            part[c, xx, rows, :] = part[c, xx, rows, :] + relay_in[rows, :]
            send(*one_step(h, n, n, to))
    load_s.wait()
    st_high[...], st_low[...] = split(s_own[...].T)
    acc[LIVE:HELD, :] = jnp.zeros((HELD - LIVE, 128), F32)

    def piece(half, owner):
        return pl.ds(pl.multiple_of(half * (HELD // 2) + owner * PIECE, 8), PIECE)

    along = (("z", z, z_in, z_s, z_r), ("y", y, y_in, y_s, y_r))
    for h, (axis, me, box, ss, rs) in enumerate(along):
        rows = PARTS[h]
        for way, n in ((0, 1), (1, 0), (0, 0), (1, 1)):
            copy(*one_step(h, way, n)).wait_recv()
        acc[rows, :] = part[c, x, rows, :] + (x_in[0, rows, :] + x_in[1, rows, :])
        for k in (4, 3, 5, 2, 6, 1, 7):
            to, device = other(axis, k)
            send(acc.at[piece(h, to)], box.at[k - 1], ss.at[k - 1], rs.at[k - 1], device)
    cross = (("y", y, zy, zy_s, zy_r), ("z", z, yz, yz_s, yz_r))
    for h, (axis, me, box, ss, rs) in enumerate(along):
        for k in range(1, 8):
            copy(acc.at[piece(h, me)], box.at[k - 1], ss.at[k - 1], rs.at[k - 1]).wait_recv()
        total = acc[piece(h, me), :]
        for k in range(1, 8):
            total += box[k - 1]
        axis, me, box, ss, rs = cross[h]
        box[me] = total
        for k in (4, 3, 5, 2, 6, 1, 7):
            send(box.at[me], box.at[me], ss.at[k - 1], rs.at[me], other(axis, k)[1])
    mine = gath.at[c, x]
    back = (("z", z, zg_s, zg_r), ("y", y, yg_s, yg_r))
    for h, (axis, me, box, ss, rs) in enumerate(cross):
        for k in range(1, 8):
            at, _ = other(axis, k)
            copy(box.at[at], box.at[at], ss.at[k - 1], rs.at[at]).wait_recv()
        total = box[0]
        for k in range(1, 8):
            total += box[k]
        axis, me, ss, rs = back[h]
        gath[c, x, piece(h, me), :] = total
        for k in (4, 3, 5, 2, 6, 1, 7):
            send(mine.at[piece(h, me)], mine.at[piece(h, me)], ss.at[k - 1], rs.at[me], other(axis, k)[1])
    def halve(core, xx, h):
        share = core * NX + xx
        for n in range(PARTS[h].size // 16):
            row = PARTS[h].start + 16 * n
            high[share, row:row + 16, :], low[share, row:row + 16, :] = split(gath[core, xx, row:row + 16, :])

    def whole(h, xx):
        ref = gath.at[c, xx, PARTS[h]]
        return ref, ref, fw_s.at[h, xx], fw_r.at[h, xx], sibling

    for h, (axis, me, ss, rs) in enumerate(back):
        for k in range(1, 8):
            at, _ = other(axis, k)
            copy(mine.at[piece(h, at)], mine.at[piece(h, at)], ss.at[k - 1], rs.at[at]).wait_recv()
        rows = PARTS[h]
        for k in (2, 1, 3):
            send(mine.at[rows], mine.at[rows], xg_s.at[h, k - 1], xg_r.at[h, x], other("x", k)[1])
        send(*whole(h, x))
        halve(c, x, h)
    for h, rows in enumerate(PARTS):
        for xx in (left, right, across):
            came = gath.at[c, xx, rows]
            copy(came, came, xg_s.at[h, 0], xg_r.at[h, xx]).wait_recv()
            send(*whole(h, xx))
            halve(c, xx, h)
    for h, rows in enumerate(PARTS):
        for xx in (x, left, right, across):
            came = gath.at[1 - c, xx, rows]
            copy(came, came, fw_s.at[h, xx], fw_r.at[h, xx]).wait_recv()
            halve(1 - c, xx, h)
    for d in sent:
        d.wait_send()


def dma(*shape):
    return pltpu.SemaphoreType.DMA(shape)


def reduced_gram(matrix, sketch):
    rows, cols = matrix.shape
    vmem = pl.BlockSpec(memory_space=pltpu.VMEM)
    return pl.pallas_call(
        reduce_kernel,
        out_shape=[jax.ShapeDtypeStruct((2 * NX, LIVE, 128), BF16)] * 2 + [jax.ShapeDtypeStruct(sketch.shape[::-1], BF16)] * 2,
        in_specs=[pl.BlockSpec(memory_space=pltpu.HBM)] * 2,
        out_specs=[vmem] * 4,
        scratch_shapes=[
            pltpu.VMEM((rows, cols), F32),
            pltpu.VMEM(sketch.shape, F32),
            pltpu.VMEM((2, NX, HELD, 128), F32),
            pltpu.VMEM((NX, LIVE, 128), F32),
            pltpu.VMEM((LIVE, 128), F32),
            pltpu.VMEM((2, LIVE, 128), F32),
            pltpu.VMEM((HELD, 128), F32),
            pltpu.VMEM((7, PIECE, 128), F32),
            pltpu.VMEM((7, PIECE, 128), F32),
            pltpu.VMEM((8, PIECE, 128), F32),
            pltpu.VMEM((8, PIECE, 128), F32),
            pltpu.VMEM((2, NX, HELD, 128), F32),
            pltpu.SemaphoreType.REGULAR,
            dma(2),
            dma(2, 4), dma(2, 4), dma(2, 2), dma(2, 2), dma(2, 2, 2), dma(2, 2, 2), dma(7), dma(7), dma(7), dma(7),
            dma(7), dma(8), dma(7), dma(8), dma(7), dma(8), dma(7), dma(8),
            dma(2, 3), dma(2, 4), dma(2, 4), dma(2, 4),
        ],
        compiler_params=pltpu.CompilerParams(collective_id=0, has_side_effects=True,
                                             vmem_limit_bytes=103 * 512 * 1024),
        name="reduce_gram",
    )(matrix, sketch)


def spread(v):
    return jnp.broadcast_to(v, (8, 128))


def eliminate(w, at):
    n8 = w.shape[0] // 8
    lanes = range(w.shape[1] // 128)
    groups = [[w[8 * g:8 * g + 8, 128 * v:128 * v + 128] for v in lanes] for g in range(n8)]
    sub = lax.broadcasted_iota(jnp.int32, (8, 128), 0)
    out = []
    for g in range(n8):
        base = at + 8 * g
        cols = {h: [spread(groups[h][0][:, base + k:base + k + 1]) for k in range(8)] for h in range(g, n8)}
        pairs = []
        for k in range(0, 8, 2):
            e0 = {m: spread(cols[g][m][k:k + 1, :]) for m in range(k, 8)}
            e1 = {m: spread(cols[g][m][k + 1:k + 2, :]) for m in range(k + 1, 8)}
            a, b, c = e0[k], e0[k + 1], e1[k + 1]
            det = a * c - b * b
            inv = 1.0 / det
            pairs.append((a, b, det))
            v0 = {m: (c * e0[m] - b * e1[m]) * inv for m in range(k + 2, 8)}
            v1 = {m: (a * e1[m] - b * e0[m]) * inv for m in range(k + 2, 8)}
            u = []
            for v in lanes:
                r0, r1 = spread(groups[g][v][k:k + 1, :]), spread(groups[g][v][k + 1:k + 2, :])
                u.append(((c * r0 - b * r1) * inv, (a * r1 - b * r0) * inv))
            for h in range(g, n8):
                c0, c1 = cols[h][k], cols[h][k + 1]
                if h == g:
                    if k == 6:
                        continue
                    c0, c1 = jnp.where(sub > k + 1, c0, 0.0), jnp.where(sub > k + 1, c1, 0.0)
                for m in range(k + 2, 8):
                    cols[h][m] = cols[h][m] - (c0 * v0[m] + c1 * v1[m])
                for v in lanes:
                    groups[h][v] = groups[h][v] - (c0 * u[v][0] + c1 * u[v][1])
        less, scale = jnp.zeros((8, 128), F32), jnp.zeros((8, 128), F32)
        for i, (a, b, det) in enumerate(pairs):
            root = lax.rsqrt(a)
            less = jnp.where(sub == 2 * i + 1, b / a, less)
            scale = jnp.where(sub == 2 * i, root, jnp.where(sub == 2 * i + 1, a * root * lax.rsqrt(det), scale))
        out.append(jnp.concatenate([(p - less * pltpu.roll(p, 1, 0)) * scale for p in groups[g]], 1))
    return jnp.concatenate(out, 0)


def cholesky_inverse(gram, work, use):
    n, nb = gram.shape[0], 64
    same = lax.broadcasted_iota(jnp.int32, (n, n), 0) == lax.broadcasted_iota(jnp.int32, (n, n), 1)
    diagonal = jnp.where(same, gram, 0.0)
    unit = lax.rsqrt(jnp.sum(diagonal, 0, keepdims=True))
    work[:, 0:n] = gram * unit * lax.rsqrt(jnp.sum(diagonal, 1, keepdims=True))
    work[:, n:] = jnp.where(same, 1.0, 0.0)
    for lo in range(0, n, nb):
        hi = lo + nb
        first, last = lo // 128 * 128, -(-hi // 128) * 128
        rows = eliminate(jnp.concatenate([work[lo:hi, first:n], work[lo:hi, n:n + last]], 1), lo - first)
        if hi < n:
            begin = hi // 128 * 128
            halves = split(rows)
            if begin > first:
                halves = tuple(v[:, begin - first:] for v in halves)
            for top in (hi,) if hi + nb == n else (hi, hi + nb):
                end = hi + nb if top == hi else n
                left = tuple(v[:, top - begin:end - begin] for v in halves)
                less = dot3(left, halves, TN)
                work[top:end, begin:n] = work[top:end, begin:n] - less[:, 0:n - begin]
                work[top:end, n:n + last] = work[top:end, n:n + last] - less[:, n - begin:]
        use(lo, rows[:, n - first:] * unit[:, 0:last])


def upper(ref, i, j):
    at = 128 * BLOCKS.index((i, j))
    return ref[at:at + 128, :]


def gram_strips(ref, corners):
    strips = []
    for s in range(3):
        p, q = 2 * s, 2 * s + 1
        above = [jnp.concatenate([upper(ref, i, p), upper(ref, i, q)], 1) for i in range(q)]
        above.append(jnp.concatenate([corners[s], upper(ref, q, q)], 1))
        right = None
        if s < 2:
            right = jnp.concatenate([jnp.concatenate([upper(ref, i, j) for j in range(q + 1, 6)], 1) for i in (p, q)], 0)
        strips.append((jnp.concatenate(above, 0), right))
    return strips


def times_gram(left, high, low):
    out = []
    for s in range(3):
        hi = 256 * s + 256
        strip = dot3((left[0][:, :hi], left[1][:, :hi]), (high[s][0], low[s][0]), NN)
        if s < 2:
            strip += dot3((left[0][:, hi:], left[1][:, hi:]), (high[s][1], low[s][1]), NT)
        out.append(strip)
    return jnp.concatenate(out, 1)


def finish_kernel(scale, g_high, g_low, st_high, st_low, a_hbm, basis_ref, coeffs_ref, work, a_own, load_sem):
    load = pltpu.make_async_copy(a_hbm, a_own, load_sem)
    load.start()
    r = lax.axis_index("rows")
    high, low = (gram_strips(ref, [upper(ref, 2 * s, 2 * s + 1).T for s in range(3)]) for ref in (g_high, g_low))
    power = split(times_gram((st_high[...], st_low[...]), high, low))
    ranged = times_gram(power, high, low)
    halves = split(ranged)
    gram = dot3(halves, power, NT)
    width = coeffs_ref.shape[0]
    row = lax.broadcasted_iota(jnp.int32, (128, 768), 0)
    col = lax.broadcasted_iota(jnp.int32, (128, 768), 1)
    pick = jnp.where(col == row + r * width, 1.0, 0.0).astype(BF16)
    rest = (ranged - halves[0].astype(F32)) - halves[1].astype(F32)
    mine = split(sum(lax.dot_general(pick, part, NT, preferred_element_type=F32)
                     for part in (halves[0], halves[1], rest.astype(BF16))))
    load.wait()
    range_rows = split(dot3(split(a_own[...]), power, NT) * scale)

    def use(lo, rows):
        nb, last = rows.shape
        factor = split(rows)
        for out, left in ((basis_ref, range_rows), (coeffs_ref, mine)):
            value = dot3((left[0][:, 0:last], left[1][:, 0:last]), factor, NT)
            out[:, lo:lo + nb] = value[0:out.shape[0], :]

    cholesky_inverse(gram, work, use)


def finish(operands, scale, width):
    vmem = pl.BlockSpec(memory_space=pltpu.VMEM)
    return pl.pallas_call(
        functools.partial(finish_kernel, scale),
        out_shape=(jax.ShapeDtypeStruct((256, 256), F32), jax.ShapeDtypeStruct((width, 256), F32)),
        in_specs=[vmem] * 4 + [pl.BlockSpec(memory_space=pltpu.HBM)],
        out_specs=(vmem, vmem),
        scratch_shapes=[
            pltpu.VMEM((256, 512), F32),
            pltpu.VMEM((256, 768), F32),
            pltpu.SemaphoreType.DMA,
        ],
        compiler_params=pltpu.CompilerParams(vmem_limit_bytes=40 * 1024 * 1024),
        name="finish",
    )(*operands)


def shards(matrix, sketch):
    parts = lax.axis_size("rows") * lax.axis_size("grp")
    high, low, *rest = reduced_gram(matrix, sketch)
    scale = float((matrix.shape[0] * parts) ** 0.5)
    width = matrix.shape[1] // lax.axis_size("rows")
    basis, coeffs = finish((high.reshape(-1, 128), low.reshape(-1, 128), *rest, matrix), scale, width)
    return basis, coeffs.T


def solution(mesh):
    return jax.shard_map(
        shards,
        mesh=mesh,
        in_specs=(P(("rows", "grp"), None), P()),
        out_specs=(P(("rows", "grp"), None), P(None, "rows")),
        check_vma=False,
    )
```

```python
import functools
import jax
import jax.numpy as jnp
from jax import lax
from jax.experimental import pallas as pl
from jax.experimental.pallas import tpu as pltpu
from jax.sharding import PartitionSpec as P

MESH = pl.DeviceIdType.MESH
F32 = jnp.float32
BF16 = jnp.bfloat16
NX, NY, NZ = 4, 8, 8
BLOCKS = [(i, j) for i in range(6) for j in range(i, 6)]
LIVE = 336
HELD = 384
PIECE = 24


def split(v):
    high = v.astype(BF16)
    return high, (v - high.astype(F32)).astype(BF16)


NN = (((1,), (0,)), ((), ()))
NT = (((1,), (1,)), ((), ()))
TN = (((0,), (0,)), ((), ()))


def dot3(left, right, dims):
    def one(a, b):
        return lax.dot_general(a, b, dims, preferred_element_type=F32)
    return one(left[0], right[1]) + one(left[1], right[0]) + one(left[0], right[0])


def place(tile):
    share, row = divmod(tile, LIVE // 8)
    return share // NX, share % NX, row * 8


def store_block(part, index, value):
    for t in range(16):
        core, x, row = place(index * 16 + t)
        part[core, x, row:row + 8, :] = value[8 * t:8 * t + 8, :]


PARTS = (pl.ds(0, HELD // 2), pl.ds(HELD // 2, LIVE - HELD // 2))
SUBS = tuple((pl.ds(p.start, p.size // 2), pl.ds(p.start + p.size // 2, p.size // 2)) for p in PARTS)


def reduce_kernel(a_hbm, s_hbm, high, low, st_high, st_low, a_own, s_own, part, sib_in, relay_in, x_in, acc, z_in, y_in, zy, yz, gath, hand, load_sem,
                  sib_s, sib_r, rl_s, rl_r, x_s, x_r, z_s, z_r, y_s, y_r, zy_s, zy_r, yz_s, yz_r,
                  zg_s, zg_r, yg_s, yg_r, xg_s, xg_r, fw_s, fw_r):
    r = lax.axis_index("rows")
    y = lax.axis_index("grp")
    x, z, c = r // 16, lax.rem(r // 2, 8), lax.rem(r, 2)

    def dev(xx, yy, zz, cc):
        return ((xx * NZ + zz) * 2 + cc, yy)

    def other(axis, k):
        if axis == "x":
            return lax.rem(x + k, NX), dev(lax.rem(x + k, NX), y, z, c)
        if axis == "y":
            return lax.rem(y + k, NY), dev(x, lax.rem(y + k, NY), z, c)
        return lax.rem(z + k, NZ), dev(x, y, lax.rem(z + k, NZ), c)

    sibling = dev(x, y, z, 1 - c)
    load = pltpu.make_async_copy(a_hbm, a_own, load_sem.at[0])
    load.start()
    barrier = pltpu.get_barrier_semaphore()

    @pl.when(c == 1)
    def _():
        pl.semaphore_signal(barrier, inc=1, device_id=sibling, device_id_type=MESH)

    @pl.when(c == 0)
    def _():
        pl.semaphore_wait(barrier, 1)
        pl.semaphore_signal(hand, inc=1, device_id=sibling, device_id_type=MESH)

    @pl.when(c == 1)
    def _():
        pl.semaphore_wait(hand, 1)
        for axis, n in (("x", NX), ("y", NY), ("z", NZ)):
            for k in range(1, n):
                pl.semaphore_signal(barrier, inc=1, device_id=other(axis, k)[1], device_id_type=MESH)

    load_s = pltpu.make_async_copy(s_hbm, s_own, load_sem.at[1])
    load_s.start()

    def copy(src, dst, s, rr, to=sibling):
        return pltpu.make_async_remote_copy(src_ref=src, dst_ref=dst, send_sem=s, recv_sem=rr,
                                            device_id=to, device_id_type=MESH)

    sent = []

    def send(*args):
        d = copy(*args)
        d.start()
        sent.append(d)

    load.wait()
    halves = split(a_own[...])
    for i in range(6):
        lo = 128 * i
        strip = dot3((halves[0][:, lo:lo + 128], halves[1][:, lo:lo + 128]), (halves[0][:, lo:], halves[1][:, lo:]), TN)
        for j in range(i, 6):
            store_block(part, BLOCKS.index((i, j)), strip[:, 128 * j - lo:128 * j - lo + 128])

    right, to_right = other("x", 1)
    left, to_left = other("x", 3)
    across, _ = other("x", 2)
    for h, xx in [(h, xx) for group in ((across,), (right, left), (x,)) for h in range(2) for xx in group]:
        rows = PARTS[h]
        send(part.at[1 - c, xx, rows], sib_in.at[xx, rows], sib_s.at[h, xx], sib_r.at[h, xx], sibling)

    def add_sibling(h, xx):
        rows = PARTS[h]
        copy(part.at[1 - c, xx, rows], sib_in.at[xx, rows], sib_s.at[h, xx], sib_r.at[h, xx]).wait_recv()
        part[c, xx, rows, :] = part[c, xx, rows, :] + sib_in[xx, rows, :]

    def relay(h, n, to=sibling):
        rows = SUBS[h][n]
        return part.at[c, across, rows], relay_in.at[rows], rl_s.at[h, n], rl_r.at[h, n], to

    def one_step(h, way, n, to=sibling):
        rows = SUBS[h][n]
        return part.at[c, (right, left)[way], rows], x_in.at[way, rows], x_s.at[h, way, n], x_r.at[h, way, n], to

    @pl.when(c == 1)
    def _():
        pl.semaphore_wait(barrier, (NX - 1) + (NY - 1) + (NZ - 1))
        pl.semaphore_signal(hand, inc=1, device_id=sibling, device_id_type=MESH)

    @pl.when(c == 0)
    def _():
        pl.semaphore_wait(hand, 1)

    for h in range(2):
        add_sibling(h, across)
        send(*relay(h, 0, to_right))
        send(*relay(h, 1, to_left))
    for h in range(2):
        add_sibling(h, right)
        send(*one_step(h, 0, 1, to_right))
        add_sibling(h, left)
        send(*one_step(h, 1, 0, to_left))
    for h in range(2):
        add_sibling(h, x)
    for h in range(2):
        for n, (xx, to) in enumerate(((right, to_right), (left, to_left))):
            rows = SUBS[h][n]
            copy(*relay(h, n)).wait_recv()
            part[c, xx, rows, :] = part[c, xx, rows, :] + relay_in[rows, :]
            send(*one_step(h, n, n, to))
    load_s.wait()
    st_high[...], st_low[...] = split(s_own[...].T)
    acc[LIVE:HELD, :] = jnp.zeros((HELD - LIVE, 128), F32)

    def piece(half, owner):
        return pl.ds(pl.multiple_of(half * (HELD // 2) + owner * PIECE, 8), PIECE)

    along = (("z", z, z_in, z_s, z_r), ("y", y, y_in, y_s, y_r))
    for h, (axis, me, box, ss, rs) in enumerate(along):
        rows = PARTS[h]
        for way, n in ((0, 1), (1, 0), (0, 0), (1, 1)):
            copy(*one_step(h, way, n)).wait_recv()
        acc[rows, :] = part[c, x, rows, :] + (x_in[0, rows, :] + x_in[1, rows, :])
        for k in (4, 3, 5, 2, 6, 1, 7):
            to, device = other(axis, k)
            send(acc.at[piece(h, to)], box.at[k - 1], ss.at[k - 1], rs.at[k - 1], device)
    cross = (("y", y, zy, zy_s, zy_r), ("z", z, yz, yz_s, yz_r))
    for h, (axis, me, box, ss, rs) in enumerate(along):
        for k in range(1, 8):
            copy(acc.at[piece(h, me)], box.at[k - 1], ss.at[k - 1], rs.at[k - 1]).wait_recv()
        total = acc[piece(h, me), :]
        for k in range(1, 8):
            total += box[k - 1]
        axis, me, box, ss, rs = cross[h]
        box[me] = total
        for k in (4, 3, 5, 2, 6, 1, 7):
            send(box.at[me], box.at[me], ss.at[k - 1], rs.at[me], other(axis, k)[1])
    mine = gath.at[c, x]
    back = (("z", z, zg_s, zg_r), ("y", y, yg_s, yg_r))
    for h, (axis, me, box, ss, rs) in enumerate(cross):
        for k in range(1, 8):
            at, _ = other(axis, k)
            copy(box.at[at], box.at[at], ss.at[k - 1], rs.at[at]).wait_recv()
        total = box[0]
        for k in range(1, 8):
            total += box[k]
        axis, me, ss, rs = back[h]
        gath[c, x, piece(h, me), :] = total
        for k in (4, 3, 5, 2, 6, 1, 7):
            send(mine.at[piece(h, me)], mine.at[piece(h, me)], ss.at[k - 1], rs.at[me], other(axis, k)[1])
    def halve(core, xx, h):
        share = core * NX + xx
        for n in range(PARTS[h].size // 16):
            row = PARTS[h].start + 16 * n
            high[share, row:row + 16, :], low[share, row:row + 16, :] = split(gath[core, xx, row:row + 16, :])

    def whole(h, xx):
        ref = gath.at[c, xx, PARTS[h]]
        return ref, ref, fw_s.at[h, xx], fw_r.at[h, xx], sibling

    for h, (axis, me, ss, rs) in enumerate(back):
        for k in range(1, 8):
            at, _ = other(axis, k)
            copy(mine.at[piece(h, at)], mine.at[piece(h, at)], ss.at[k - 1], rs.at[at]).wait_recv()
        rows = PARTS[h]
        for k in (2, 1, 3):
            send(mine.at[rows], mine.at[rows], xg_s.at[h, k - 1], xg_r.at[h, x], other("x", k)[1])
        send(*whole(h, x))
        halve(c, x, h)
    for h, rows in enumerate(PARTS):
        for xx in (left, right, across):
            came = gath.at[c, xx, rows]
            copy(came, came, xg_s.at[h, 0], xg_r.at[h, xx]).wait_recv()
            send(*whole(h, xx))
            halve(c, xx, h)
    for h, rows in enumerate(PARTS):
        for xx in (x, left, right, across):
            came = gath.at[1 - c, xx, rows]
            copy(came, came, fw_s.at[h, xx], fw_r.at[h, xx]).wait_recv()
            halve(1 - c, xx, h)
    for d in sent:
        d.wait_send()


def dma(*shape):
    return pltpu.SemaphoreType.DMA(shape)


def reduced_gram(matrix, sketch):
    rows, cols = matrix.shape
    vmem = pl.BlockSpec(memory_space=pltpu.VMEM)
    return pl.pallas_call(
        reduce_kernel,
        out_shape=[jax.ShapeDtypeStruct((2 * NX, LIVE, 128), BF16)] * 2 + [jax.ShapeDtypeStruct(sketch.shape[::-1], BF16)] * 2,
        in_specs=[pl.BlockSpec(memory_space=pltpu.HBM)] * 2,
        out_specs=[vmem] * 4,
        scratch_shapes=[
            pltpu.VMEM((rows, cols), F32),
            pltpu.VMEM(sketch.shape, F32),
            pltpu.VMEM((2, NX, HELD, 128), F32),
            pltpu.VMEM((NX, LIVE, 128), F32),
            pltpu.VMEM((LIVE, 128), F32),
            pltpu.VMEM((2, LIVE, 128), F32),
            pltpu.VMEM((HELD, 128), F32),
            pltpu.VMEM((7, PIECE, 128), F32),
            pltpu.VMEM((7, PIECE, 128), F32),
            pltpu.VMEM((8, PIECE, 128), F32),
            pltpu.VMEM((8, PIECE, 128), F32),
            pltpu.VMEM((2, NX, HELD, 128), F32),
            pltpu.SemaphoreType.REGULAR,
            dma(2),
            dma(2, 4), dma(2, 4), dma(2, 2), dma(2, 2), dma(2, 2, 2), dma(2, 2, 2), dma(7), dma(7), dma(7), dma(7),
            dma(7), dma(8), dma(7), dma(8), dma(7), dma(8), dma(7), dma(8),
            dma(2, 3), dma(2, 4), dma(2, 4), dma(2, 4),
        ],
        compiler_params=pltpu.CompilerParams(collective_id=0, has_side_effects=True,
                                             vmem_limit_bytes=103 * 512 * 1024),
        name="reduce_gram",
    )(matrix, sketch)


def spread(v):
    return jnp.broadcast_to(v, (8, 128))


def eliminate(w, at):
    n8 = w.shape[0] // 8
    lanes = range(w.shape[1] // 128)
    groups = [[w[8 * g:8 * g + 8, 128 * v:128 * v + 128] for v in lanes] for g in range(n8)]
    sub = lax.broadcasted_iota(jnp.int32, (8, 128), 0)
    out = []
    for g in range(n8):
        base = at + 8 * g
        cols = {h: [spread(groups[h][0][:, base + k:base + k + 1]) for k in range(8)] for h in range(g, n8)}
        pairs = []
        for k in range(0, 8, 2):
            e0 = {m: spread(cols[g][m][k:k + 1, :]) for m in range(k, 8)}
            e1 = {m: spread(cols[g][m][k + 1:k + 2, :]) for m in range(k + 1, 8)}
            a, b, c = e0[k], e0[k + 1], e1[k + 1]
            det = a * c - b * b
            inv = 1.0 / det
            pairs.append((a, b, det))
            v0 = {m: (c * e0[m] - b * e1[m]) * inv for m in range(k + 2, 8)}
            v1 = {m: (a * e1[m] - b * e0[m]) * inv for m in range(k + 2, 8)}
            u = []
            for v in lanes:
                r0, r1 = spread(groups[g][v][k:k + 1, :]), spread(groups[g][v][k + 1:k + 2, :])
                u.append(((c * r0 - b * r1) * inv, (a * r1 - b * r0) * inv))
            for h in range(g, n8):
                c0, c1 = cols[h][k], cols[h][k + 1]
                if h == g:
                    if k == 6:
                        continue
                    c0, c1 = jnp.where(sub > k + 1, c0, 0.0), jnp.where(sub > k + 1, c1, 0.0)
                for m in range(k + 2, 8):
                    cols[h][m] = cols[h][m] - (c0 * v0[m] + c1 * v1[m])
                for v in lanes:
                    groups[h][v] = groups[h][v] - (c0 * u[v][0] + c1 * u[v][1])
        less, scale = jnp.zeros((8, 128), F32), jnp.zeros((8, 128), F32)
        for i, (a, b, det) in enumerate(pairs):
            root = lax.rsqrt(a)
            less = jnp.where(sub == 2 * i + 1, b / a, less)
            scale = jnp.where(sub == 2 * i, root, jnp.where(sub == 2 * i + 1, a * root * lax.rsqrt(det), scale))
        out.append(jnp.concatenate([(p - less * pltpu.roll(p, 1, 0)) * scale for p in groups[g]], 1))
    return jnp.concatenate(out, 0)


def cholesky_inverse(gram, work, use):
    n, nb = gram.shape[0], 64
    same = lax.broadcasted_iota(jnp.int32, (n, n), 0) == lax.broadcasted_iota(jnp.int32, (n, n), 1)
    diagonal = jnp.where(same, gram, 0.0)
    unit = lax.rsqrt(jnp.sum(diagonal, 0, keepdims=True))
    work[:, 0:n] = gram * unit * lax.rsqrt(jnp.sum(diagonal, 1, keepdims=True))
    work[:, n:] = jnp.where(same, 1.0, 0.0)
    for lo in range(0, n, nb):
        hi = lo + nb
        first, last = lo // 128 * 128, -(-hi // 128) * 128
        rows = eliminate(jnp.concatenate([work[lo:hi, first:n], work[lo:hi, n:n + last]], 1), lo - first)
        if hi < n:
            begin = hi // 128 * 128
            halves = split(rows)
            if begin > first:
                halves = tuple(v[:, begin - first:] for v in halves)
            for top in (hi,) if hi + nb == n else (hi, hi + nb):
                end = hi + nb if top == hi else n
                left = tuple(v[:, top - begin:end - begin] for v in halves)
                less = dot3(left, halves, TN)
                work[top:end, begin:n] = work[top:end, begin:n] - less[:, 0:n - begin]
                work[top:end, n:n + last] = work[top:end, n:n + last] - less[:, n - begin:]
        use(lo, rows[:, n - first:] * unit[:, 0:last])


def upper(ref, i, j):
    at = 128 * BLOCKS.index((i, j))
    return ref[at:at + 128, :]


def gram_strips(ref, corners):
    strips = []
    for s in range(3):
        p, q = 2 * s, 2 * s + 1
        above = [jnp.concatenate([upper(ref, i, p), upper(ref, i, q)], 1) for i in range(q)]
        above.append(jnp.concatenate([corners[s], upper(ref, q, q)], 1))
        right = None
        if s < 2:
            right = jnp.concatenate([jnp.concatenate([upper(ref, i, j) for j in range(q + 1, 6)], 1) for i in (p, q)], 0)
        strips.append((jnp.concatenate(above, 0), right))
    return strips


def times_gram(left, high, low):
    out = []
    for s in range(3):
        hi = 256 * s + 256
        strip = dot3((left[0][:, :hi], left[1][:, :hi]), (high[s][0], low[s][0]), NN)
        if s < 2:
            strip += dot3((left[0][:, hi:], left[1][:, hi:]), (high[s][1], low[s][1]), NT)
        out.append(strip)
    return jnp.concatenate(out, 1)


def finish_kernel(scale, g_high, g_low, st_high, st_low, a_hbm, basis_hbm, coeffs_ref,
                  work, basis_ref, a_own, load_sem, store_sem):
    load = pltpu.make_async_copy(a_hbm, a_own, load_sem)
    load.start()
    r = lax.axis_index("rows")
    high, low = (gram_strips(ref, [upper(ref, 2 * s, 2 * s + 1).T for s in range(3)]) for ref in (g_high, g_low))
    power = split(times_gram((st_high[...], st_low[...]), high, low))
    ranged = times_gram(power, high, low)
    halves = split(ranged)
    gram = dot3(halves, power, NT)
    width = coeffs_ref.shape[0]
    row = lax.broadcasted_iota(jnp.int32, (128, 768), 0)
    col = lax.broadcasted_iota(jnp.int32, (128, 768), 1)
    pick = jnp.where(col == row + r * width, 1.0, 0.0).astype(BF16)
    rest = (ranged - halves[0].astype(F32)) - halves[1].astype(F32)
    mine = split(sum(lax.dot_general(pick, part, NT, preferred_element_type=F32)
                     for part in (halves[0], halves[1], rest.astype(BF16))))
    load.wait()
    range_rows = split(dot3(split(a_own[...]), power, NT) * scale)

    def store(n):
        columns = pl.ds(128 * n, 128)
        return pltpu.make_async_copy(basis_ref.at[:, columns], basis_hbm.at[:, columns], store_sem.at[n])

    def use(lo, rows):
        nb, last = rows.shape
        factor = split(rows)
        for out, left in ((basis_ref, range_rows), (coeffs_ref, mine)):
            value = dot3((left[0][:, 0:last], left[1][:, 0:last]), factor, NT)
            out[:, lo:lo + nb] = value[0:out.shape[0], :]
        if (lo + nb) % 128 == 0:
            store((lo + nb) // 128 - 1).start()

    cholesky_inverse(gram, work, use)
    for n in range(2):
        store(n).wait()


def finish(operands, scale, width):
    vmem = pl.BlockSpec(memory_space=pltpu.VMEM)
    return pl.pallas_call(
        functools.partial(finish_kernel, scale),
        out_shape=(jax.ShapeDtypeStruct((256, 256), F32), jax.ShapeDtypeStruct((width, 256), F32)),
        in_specs=[vmem] * 4 + [pl.BlockSpec(memory_space=pltpu.HBM)],
        out_specs=(pl.BlockSpec(memory_space=pltpu.HBM), vmem),
        scratch_shapes=[
            pltpu.VMEM((256, 512), F32),
            pltpu.VMEM((256, 256), F32),
            pltpu.VMEM((256, 768), F32),
            pltpu.SemaphoreType.DMA,
            pltpu.SemaphoreType.DMA((2,)),
        ],
        compiler_params=pltpu.CompilerParams(vmem_limit_bytes=40 * 1024 * 1024),
        name="finish",
    )(*operands)


def shards(matrix, sketch):
    parts = lax.axis_size("rows") * lax.axis_size("grp")
    high, low, *rest = reduced_gram(matrix, sketch)
    scale = float((matrix.shape[0] * parts) ** 0.5)
    width = matrix.shape[1] // lax.axis_size("rows")
    basis, coeffs = finish((high.reshape(-1, 128), low.reshape(-1, 128), *rest, matrix), scale, width)
    return basis, coeffs.T


def solution(mesh):
    return jax.shard_map(
        shards,
        mesh=mesh,
        in_specs=(P(("rows", "grp"), None), P()),
        out_specs=(P(("rows", "grp"), None), P(None, "rows")),
        check_vma=False,
    )
```
